128 devices in a mesh: gx: 32 (over y, x, core), gy: 4 (over z).
Axes of the slice: x: 4, y: 4, z: 4, core: 2. Of those that a mesh axis runs over, the one named last changes fastest.
Arguments:
- density: float32 [256, 16384], P('gx', 'gy'), may hold values from 1 to 2
- momentum: float32 [3, 256, 16384], P(None, 'gx', 'gy'), may hold values from -0.03 to 0.03
- energy: float32 [256, 16384], P('gx', 'gy'), may hold values from 4 to 6
- basis: bfloat16 [16, 3, 256, 16384], P(None, None, 'gx', 'gy'), may hold values from -4 to 4
- scales: float32 [16], replicated, may hold values from 1 to 10
- snapshots: bfloat16 [15, 3, 256, 16384], P(None, None, 'gx', 'gy'), may hold values from -720 to 720
Outputs:
- density_out: float32 [256, 16384], P('gx', 'gy')
- momentum_out: float32 [3, 256, 16384], P(None, 'gx', 'gy')
- energy_out: float32 [256, 16384], P('gx', 'gy')
- modes: bfloat16 [32, 3, 256, 16384], P(None, None, 'gx', 'gy')
- factor: float32 [32, 32], replicated
The draws below stay inside these ranges and needn't reach their ends.
All inputs are finite; a program needn't handle non-finite values.
Results may differ from the reference program's by a relative error of at most 0.001.
Values sent between devices are 32-bit elements; how exact they have to be, the bound alone decides.
No kernel may reach another device: no remote copies, remote signals or barrier semaphores. Data moves between devices by JAX's collectives and lax.ppermute only.
A program may use at most 128 MiB of HBM per device.

```python
import math
import jax
import jax.numpy as jnp
from jax import lax

CX = 8
NZ = 64
RANK = 16
SNAPS = 15
COLS = 32
NX = 256
NY = 256
ROWS = 12582912
N_GX = 32


def common_state(key):
    density = jax.random.uniform(jax.random.fold_in(key, 101), (NX, NY * NZ), jnp.float32, 1.0, 2.0)
    raw = jax.random.uniform(jax.random.fold_in(key, 102), (3, NX, NY * NZ), jnp.float32, -1.0, 1.0)
    momentum = 0.03 * jnp.clip(raw, -1.0, 1.0)
    return (density, momentum)


def draw_density(key, part):
    density, momentum = common_state(key)
    return density


def draw_momentum(key, part):
    density, momentum = common_state(key)
    return momentum


def draw_snapshots(key, part):
    density, momentum = common_state(key)
    key = jax.random.fold_in(key, 7)
    shape = (SNAPS - 1, 3, NX, NY * NZ)
    values = jax.random.normal(jax.random.fold_in(key, 1), shape, jnp.float32)
    column = jnp.exp(jax.random.uniform(jax.random.fold_in(key, 2), (SNAPS - 1, 1, 1, 1), jnp.float32, 0.0, math.log(10.0)))
    along = jnp.arange(NX, dtype=jnp.float32).reshape(1, 1, NX, 1) / NX
    rising = jnp.exp(math.log(10.0) * along)
    earlier = jnp.clip(values, -6.0, 6.0) * column * rising
    noise = jax.random.normal(jax.random.fold_in(key, 4), (1, 3, NX, NY * NZ), jnp.float32)
    previous = momentum[None] / density[None, None] + 0.003 * jnp.clip(noise, -4.0, 4.0)
    return jnp.concatenate([earlier, previous], 0).astype(jnp.bfloat16)


def steps_of(stream_key, dims, cuts, low, largest):
    def one(axis_at, shards_of):
        steps = jax.random.uniform(jax.random.fold_in(jax.random.fold_in(stream_key, 6), axis_at), (shards_of,), jnp.float32, low / len(cuts), largest / len(cuts))
        return jnp.repeat(jnp.exp(steps), dims[axis_at] // shards_of).reshape((-1,) + (1,) * (len(dims) - axis_at - 1))

    gain = one(*cuts[0])
    for cut in cuts[1:]:
        gain = gain * one(*cut)
    return gain


def scatter_about(stream_key, shape, width, reach, shards=(), kind=jnp.bfloat16):
    values = width * jax.random.normal(stream_key, shape, jnp.float32)
    if shards:
        values = values * steps_of(stream_key, shape, shards, -0.22, 0.18)
    return jnp.clip(values, -reach, reach).astype(kind)


def setup_inputs(seed: int = 0) -> dict:
    arg_keys = jax.random.split(jax.random.key(seed), 7)
    return {
        "density": draw_density(jax.random.fold_in(arg_keys[6], 71), 0),
        "momentum": draw_momentum(jax.random.fold_in(arg_keys[6], 71), 0),
        "energy": jnp.clip(4.0 + 2.0 * jax.random.uniform(arg_keys[2], (NX, NY * NZ), jnp.float32) ** steps_of(arg_keys[2], (NX, NY * NZ), ((0, 32), (1, 4)), -0.2, 0.2), 4.0, 6.0),
        "basis": scatter_about(arg_keys[3], (RANK, 3, NX, NY * NZ), 1.0, 4.0, ((2, 32), (3, 4))),
        "scales": jnp.clip(jnp.exp(jax.random.uniform(arg_keys[4], (RANK,), jnp.float32, math.log(1.0), math.log(10.0))), 1.0, 10.0),
        "snapshots": draw_snapshots(jax.random.fold_in(arg_keys[6], 71), 0),
    }


STEP_TIME = 0.03
FIRST = (0.8, -0.2, 4.0 / 105.0, -1.0 / 280.0)
LATTER_PHASE = (8.0 / 5.0, -0.2, 8.0 / 315.0, -1.0 / 560.0)
CENTRAL_COEFF = -205.0 / 72.0

def shift_depth(solution_tensors, displacement):
    column = jnp.arange(solution_tensors.shape[-1], dtype=jnp.int32) % NZ
    inside = jnp.roll(solution_tensors, -displacement, axis=-1)
    amount = NZ - displacement if displacement > 0 else -displacement - NZ
    wrapped = jnp.roll(solution_tensors, amount, axis=-1)
    keep = (column + displacement >= 0) & (column + displacement < NZ)
    return jnp.where(keep, inside, wrapped)

def basic_unknowns(solution_tensors):
    flow_speed_grid = solution_tensors[1:4] / solution_tensors[0]
    normal_stress_grid = 0.4 * (solution_tensors[4] - 0.5 * lax.optimization_barrier(jnp.sum(solution_tensors[1:4] * flow_speed_grid, axis=0)))
    thermal_grid = normal_stress_grid / solution_tensors[0]
    return (flow_speed_grid, normal_stress_grid, thermal_grid)

def pointwise(solution_tensors, direction):
    flow_speed_grid, normal_stress_grid, thermal_grid = basic_unknowns(solution_tensors)
    moving = flow_speed_grid[direction]
    unit_vector = (jnp.arange(3) == direction).astype(jnp.float32).reshape(3, 1, 1)
    mass_transport = solution_tensors[1 + direction]
    momentum_transport = solution_tensors[1:4] * moving + unit_vector * normal_stress_grid
    energy_transport = (solution_tensors[4] + normal_stress_grid) * moving
    face_exchange_list = jnp.concatenate([mass_transport[None], momentum_transport, energy_transport[None]], 0)
    return (face_exchange_list, flow_speed_grid, thermal_grid)

def tendency(solution_tensors, neighbour):
    flow_speed_grid, normal_stress_grid, thermal_grid = basic_unknowns(solution_tensors)
    shear_resistance = 0.08 * thermal_grid
    diffused_flow_speed = 3.0 * CENTRAL_COEFF * flow_speed_grid
    thermal_curvature = 3.0 * CENTRAL_COEFF * thermal_grid
    divergence = jnp.zeros_like(solution_tensors)
    for direction in range(3):
        for displacement in range(4):
            plus_flux, plus_vel, upper_neighbor_heat = pointwise(neighbour(direction, displacement + 1), direction)
            minus_flux, minus_vel, lower_neighbor_heat = pointwise(neighbour(direction, -displacement - 1), direction)
            divergence = divergence + FIRST[displacement] * (plus_flux - minus_flux)
            diffused_flow_speed = diffused_flow_speed + LATTER_PHASE[displacement] * (plus_vel + minus_vel)
            thermal_curvature = thermal_curvature + LATTER_PHASE[displacement] * (upper_neighbor_heat + lower_neighbor_heat)
    thermal_source = shear_resistance * (lax.optimization_barrier(jnp.sum(flow_speed_grid * diffused_flow_speed, axis=0)) + 4.9 * thermal_curvature)
    viscous = jnp.concatenate([jnp.zeros_like(thermal_source)[None], shear_resistance * diffused_flow_speed, thermal_source[None]], 0)
    return viscous - divergence

def advance(solution_tensors, rate):
    first = solution_tensors + STEP_TIME * rate(solution_tensors)
    second = 0.75 * solution_tensors + 0.25 * (first + STEP_TIME * rate(first))
    return solution_tensors / 3.0 + 2.0 / 3.0 * (second + STEP_TIME * rate(second))

def upper_factor(gram):
    extent = gram.shape[0]
    position = jnp.arange(extent, dtype=jnp.int32)

    def eliminate(column_index, carry):
        remainder, result = carry
        pivot_row = lax.dynamic_index_in_dim(remainder, column_index, 0, keepdims=False)
        pivot_value = jnp.sqrt(lax.dynamic_index_in_dim(pivot_row, column_index, 0, keepdims=False))
        scaled = jnp.where(position >= column_index, pivot_row / pivot_value, jnp.zeros_like(pivot_row))
        remainder = remainder - scaled[:, None] * scaled[None, :]
        result = lax.dynamic_update_index_in_dim(result, scaled, column_index, 0)
        return (remainder, result)
    return lax.fori_loop(0, extent, eliminate, (gram, jnp.zeros_like(gram)))[1]

def upper_inverse(factor):
    extent = factor.shape[0]
    position = jnp.arange(extent, dtype=jnp.int32)
    identity_matrix = jnp.eye(extent, dtype=factor.dtype)

    def backward(counter, inverse):
        row_index = extent - 1 - counter
        factor_row = lax.dynamic_index_in_dim(factor, row_index, 0, keepdims=False)
        diagonal_value = lax.dynamic_index_in_dim(factor_row, row_index, 0, keepdims=False)
        strict = jnp.where(position > row_index, factor_row, jnp.zeros_like(factor_row))
        target = lax.dynamic_index_in_dim(identity_matrix, row_index, 0, keepdims=False)
        solved = (target - jnp.dot(strict, inverse, precision=lax.Precision.HIGHEST)) / diagonal_value
        return lax.dynamic_update_index_in_dim(inverse, solved, row_index, 0)
    return lax.fori_loop(0, extent, backward, jnp.zeros_like(factor))

def reference(density, momentum, energy, basis, scales, snapshots):
    solution_tensors = jnp.concatenate([density[None], momentum, energy[None]], 0)

    def rate(current_solution):

        def neighbour(direction, displacement):
            if direction == 0:
                return jnp.roll(current_solution, -displacement, axis=1)
            if direction == 1:
                return jnp.roll(current_solution, -displacement * NZ, axis=2)
            return shift_depth(current_solution, displacement)
        return tendency(current_solution, neighbour)
    solution_tensors = advance(solution_tensors, rate)
    newest = solution_tensors[1:4] / solution_tensors[0]

    def block_columns(block_index):
        start = (block_index * CX).astype(jnp.int32)
        basis_part = lax.dynamic_slice_in_dim(basis, start, CX, 2).astype(jnp.float32)
        snap_part = lax.dynamic_slice_in_dim(snapshots, start, CX, 2).astype(jnp.float32)
        new_part = lax.dynamic_slice_in_dim(newest, start, CX, 1)
        return jnp.concatenate([basis_part * scales[:, None, None, None], snap_part, new_part[None]], 0)

    def add_block(block_index, total):
        columns = block_columns(block_index)
        return total + jnp.einsum('kabc,jabc->kj', columns, columns, precision=lax.Precision.HIGHEST)
    gram = lax.fori_loop(0, N_GX, add_block, jnp.zeros((COLS, COLS), jnp.float32))
    factor = upper_factor(1.0 / ROWS * gram)
    inverse = upper_inverse(factor)

    def write_block(block_index, modes):
        columns = block_columns(block_index)
        part = jnp.einsum('kj,kabc->jabc', inverse, columns, precision=lax.Precision.HIGHEST).astype(jnp.bfloat16)
        start = (block_index * CX).astype(jnp.int32)
        return lax.dynamic_update_slice_in_dim(modes, part, start, 2)
    modes = lax.fori_loop(0, N_GX, write_block, jnp.zeros((COLS, 3, NX, NY * NZ), jnp.bfloat16))
    return (solution_tensors[0], solution_tensors[1:4], solution_tensors[4], modes, factor)
```

```python
import functools

import jax
import jax.numpy as jnp
from jax import lax
from jax.experimental import pallas as pl
from jax.experimental.pallas import tpu as pltpu
from jax.sharding import PartitionSpec as P

NZ = 64
LANES = 128
STEP_TIME = 0.03
FIRST = (0.8, -0.2, 4.0 / 105.0, -1.0 / 280.0)
SECOND = (8.0 / 5.0, -0.2, 8.0 / 315.0, -1.0 / 560.0)
CENTRAL = -205.0 / 72.0
VMEM_LIMIT = 48 * 1024 * 1024
WHOLE = pl.BlockSpec(memory_space=pltpu.VMEM)


def lanes_at(index):
    return pl.ds(pl.multiple_of(index * LANES, LANES), LANES)


def row_ids():
    return lax.broadcasted_iota(jnp.int32, (8, LANES), 0)


def lane_ids():
    return lax.broadcasted_iota(jnp.int32, (8, LANES), 1)


def primitives(rho, mx, my, mz, energy):
    inv = 1.0 / rho
    u, v, w = mx * inv, my * inv, mz * inv
    p = 0.4 * (energy - 0.5 * (mx * u + my * v + mz * w))
    return u, v, w, p, p * inv


def pack_sends(state, to_below, to_above, first_y, last_y):
    length = state[0].shape[-1]
    half = length // (2 * LANES)
    low = row_ids() < 4

    def body(j, carry):
        for f in range(5):
            here = state[f][:, lanes_at(j)]
            other = pltpu.roll(state[f][:, lanes_at(j + half)], 4, 0)
            to_below[f, :, lanes_at(j)] = jnp.where(low, here, other)
            to_above[f, :, lanes_at(j)] = jnp.where(low, other, here)
        return carry

    lax.fori_loop(0, half, body, 0)
    width = 4 * NZ
    for f in range(5):
        first_y[f] = state[f][:, :width]
        last_y[f] = state[f][:, length - width :]


def state_views(rho, mom, energy):
    return [rho, mom.at[0], mom.at[1], mom.at[2], energy]


def pack_kernel(rho, mom, energy, to_below, to_above, first_y, last_y):
    pack_sends(state_views(rho, mom, energy), to_below, to_above, first_y, last_y)


def stage_kernel(stage, refs):
    if stage == 0:
        rho, mom, energy, above, below, before, after = refs[:7]
        base = None
        rest = refs[7:]
    else:
        rho, mom, energy, rho0, mom0, energy0, above, below, before, after = refs[:10]
        base = state_views(rho0, mom0, energy0)
        rest = refs[10:]
    if stage < 2:
        rho_o, mom_o, energy_o, to_below, to_above, first_y, last_y = rest[:7]
        ys, yh, hx = rest[7:]
    else:
        rho_o, mom_o, energy_o, newest = rest[:4]
        ys, yh, hx = rest[4:]
    state = state_views(rho, mom, energy)
    outs = state_views(rho_o, mom_o, energy_o)
    length = rho.shape[-1]
    blocks = length // LANES
    half = blocks // 2
    row, lane = row_ids(), lane_ids()
    depth = lane % NZ
    low = row < 4

    def fill(fields, block):
        r, mx, my, mz, e = fields
        u, v, w, p, t = primitives(r, mx, my, mz, e)
        at = lanes_at(block)
        for f, value in enumerate(
            (my, mx * v, my * v + p, mz * v, (e + p) * v, u, v, w, t, p)
        ):
            ys[f, :, at] = value

    def fill_own(j, carry):
        fill([s[:, lanes_at(j)] for s in state], j + 2)
        return carry

    lax.fori_loop(0, blocks, fill_own, 0)
    for j in range(2):
        fill([before[f, :, j * LANES : (j + 1) * LANES] for f in range(5)], j)
        fill([after[f, :, j * LANES : (j + 1) * LANES] for f in range(5)], blocks + 2 + j)

    def shift_half(j, carry):
        for f in range(9):
            here, following = ys[f, :, lanes_at(j)], ys[f, :, lanes_at(j + 1)]
            yh[f, :, lanes_at(j)] = pltpu.roll(
                jnp.where(lane < NZ, following, here), NZ, 1
            )
        return carry

    lax.fori_loop(0, blocks + 3, shift_half, 0)

    def unpack(j, carry):
        for f in range(5):
            a, b = above[f, :, lanes_at(j)], below[f, :, lanes_at(j)]
            hx[f, :, lanes_at(j)] = jnp.where(low, a, b)
            hx[f, :, lanes_at(j + half)] = pltpu.roll(jnp.where(low, b, a), 4, 0)
        return carry

    lax.fori_loop(0, half, unpack, 0)

    def main(j, carry):
        at = lanes_at(j)
        own = [s[:, at] for s in state]
        r, mx, my, mz, e = own
        u, v, w, t, p = [ys[5 + f, :, lanes_at(j + 2)] for f in range(5)]
        energy_p = e + p
        hr, hmx, hmy, hmz, he = [hx[f, :, at] for f in range(5)]
        hu, hv, hw, hp, ht = primitives(hr, hmx, hmy, hmz, he)
        fx = (mx, mx * u + p, my * u, mz * u, energy_p * u, u, v, w, t)
        hfx = (hmx, hmx * hu + hp, hmy * hu, hmz * hu, (he + hp) * hu, hu, hv, hw, ht)
        fz = (mz, mx * w, my * w, mz * w + p, energy_p * w, u, v, w, t)
        result = []
        for f in range(9):
            total = None if f < 5 else (3.0 * CENTRAL) * fx[f]
            swapped_half = pltpu.roll(fz[f], NZ, 1)
            for k in range(1, 5):
                pairs = [
                    (
                        pltpu.roll(jnp.where(row < k, hfx[f], fx[f]), 8 - k, 0),
                        pltpu.roll(jnp.where(row >= 8 - k, hfx[f], fx[f]), k, 0),
                    ),
                    (
                        pltpu.roll(
                            jnp.where(depth < k, swapped_half, fz[f]), LANES - k, 1
                        ),
                        pltpu.roll(
                            jnp.where(depth >= NZ - k, swapped_half, fz[f]), k, 1
                        ),
                    ),
                ]
                if k % 2:
                    up, down = (k - 1) // 2, -(k + 1) // 2
                    pairs.append(
                        (yh[f, :, lanes_at(j + 2 + up)], yh[f, :, lanes_at(j + 2 + down)])
                    )
                else:
                    pairs.append(
                        (
                            ys[f, :, lanes_at(j + 2 + k // 2)],
                            ys[f, :, lanes_at(j + 2 - k // 2)],
                        )
                    )
                if f < 5:
                    s = sum(a - b for a, b in pairs)
                    term = FIRST[k - 1] * s
                else:
                    s = sum(a + b for a, b in pairs)
                    term = SECOND[k - 1] * s
                total = term if total is None else total + term
            result.append(total)
        visc = 0.08 * t
        lap = result[5:]
        work = visc * (u * lap[0] + v * lap[1] + w * lap[2] + 4.9 * lap[3])
        rate = [
            -result[0],
            visc * lap[0] - result[1],
            visc * lap[1] - result[2],
            visc * lap[2] - result[3],
            work - result[4],
        ]
        final = []
        for f in range(5):
            step = own[f] + STEP_TIME * rate[f]
            if stage == 1:
                step = 0.75 * base[f][:, at] + 0.25 * step
            elif stage == 2:
                step = base[f][:, at] * (1.0 / 3.0) + (2.0 / 3.0) * step
            outs[f][:, at] = step
            final.append(step)
        if stage == 2:
            inv = 1.0 / final[0]
            for c in range(3):
                newest[c, :, at] = final[1 + c] * inv
        return carry

    lax.fori_loop(0, blocks, main, 0)
    if stage < 2:
        pack_sends(outs, to_below, to_above, first_y, last_y)


def f32(*shape):
    return jax.ShapeDtypeStruct(shape, jnp.float32)


def call(kernel, out_shape, args, scratch=(), flops=0, nbytes=0, **kw):
    return pl.pallas_call(
        kernel,
        out_shape=out_shape,
        scratch_shapes=list(scratch),
        compiler_params=pltpu.CompilerParams(vmem_limit_bytes=VMEM_LIMIT),
        cost_estimate=pl.CostEstimate(
            flops=flops, bytes_accessed=nbytes, transcendentals=0
        ),
        **kw,
    )(*args)


def state_shapes(rows, length):
    return (f32(rows, length), f32(3, rows, length), f32(rows, length))


def send_shapes(rows, length):
    packed = f32(5, rows, length // 2)
    edge = f32(5, rows, 4 * NZ)
    return (packed, packed, edge, edge)


def pack(state):
    rows, length = state[0].shape
    shapes = send_shapes(rows, length)
    return call(
        pack_kernel,
        shapes,
        state,
        in_specs=[WHOLE] * 3,
        out_specs=[WHOLE] * 4,
        nbytes=10**6,
    )


def stage_call(stage, state, base, halo):
    rows, length = state[0].shape
    out = state_shapes(rows, length)
    out += send_shapes(rows, length) if stage < 2 else (f32(3, rows, length),)
    args = tuple(state) + (tuple(base) if stage else ()) + tuple(halo)
    scratch = [
        pltpu.VMEM((10, rows, length + 8 * NZ), jnp.float32),
        pltpu.VMEM((9, rows, length + 8 * NZ), jnp.float32),
        pltpu.VMEM((5, rows, length), jnp.float32),
    ]
    return call(
        lambda *refs: stage_kernel(stage, refs),
        out,
        args,
        scratch,
        in_specs=[WHOLE] * len(args),
        out_specs=[WHOLE] * len(out),
        flops=32768 * 700,
        nbytes=3 * 10**6,
    )


def merged_rows(basis, snaps, c):
    first = basis[:, c].astype(jnp.float32)
    second = snaps[:, c].astype(jnp.float32)
    length = first.shape[-1]
    rows = jnp.concatenate([first, second, jnp.zeros((1, 8, length), jnp.float32)], 0)
    return rows.reshape(256, length).astype(jnp.bfloat16)


def group_matrix(shape, group_dim, dtype):
    g = lax.broadcasted_iota(jnp.int32, shape, group_dim)
    o = lax.broadcasted_iota(jnp.int32, shape, 1 - group_dim)
    return (g // 8 == o).astype(dtype)


def same_layer():
    r = lax.broadcasted_iota(jnp.int32, (256, 256), 0)
    c = lax.broadcasted_iota(jnp.int32, (256, 256), 1)
    return r % 8 == c % 8


def gram_kernel(basis, snaps, gram, total):
    step = pl.program_id(0)

    @pl.when(step == 0)
    def _():
        total[...] = jnp.zeros_like(total)

    for c in range(3):
        rows = merged_rows(basis, snaps, c)
        total[...] += lax.dot_general(
            rows, rows, (((1,), (1,)), ((), ())), preferred_element_type=jnp.float32
        )

    @pl.when(step == pl.num_programs(0) - 1)
    def _():
        kept = jnp.where(same_layer(), total[...], 0.0)
        left = group_matrix((32, 256), 1, jnp.float32)
        right = group_matrix((256, 32), 0, jnp.float32)
        small = jnp.dot(left, kept, precision=lax.Precision.HIGHEST)
        small = jnp.dot(small, right, precision=lax.Precision.HIGHEST)
        for g in range(4):
            gram[:, 32 * g : 32 * g + 32] = small[8 * g : 8 * g + 8]


def column_specs(width):
    return [
        pl.BlockSpec((16, 3, 8, width), lambda i: (0, 0, 0, i)),
        pl.BlockSpec((15, 3, 8, width), lambda i: (0, 0, 0, i)),
    ]


def gram_call(basis, snaps, width=1024):
    length = basis.shape[-1]
    return call(
        gram_kernel,
        f32(8, LANES),
        (basis, snaps),
        [pltpu.VMEM((256, 256), jnp.float32)],
        grid=(length // width,),
        in_specs=column_specs(width),
        out_specs=pl.BlockSpec((8, LANES), lambda i: (0, 0)),
        flops=2 * 256 * 256 * 3 * length,
        nbytes=31 * 3 * 8 * length * 2,
    )


def factor_kernel(weight, gram, scale, upper, lower, high, low):
    row = lax.broadcasted_iota(jnp.int32, (32, 32), 0)
    col = lax.broadcasted_iota(jnp.int32, (32, 32), 1)
    s = jnp.broadcast_to(scale[...], (32, 32))
    s_col = jnp.sum(jnp.where(row == col, s, 0.0), axis=1, keepdims=True)
    g = jnp.concatenate([gram[:, 32 * i : 32 * i + 32] for i in range(4)], 0)
    g = g * (weight * s) * s_col
    inside = (row < 31) & (col < 31)
    eye = (row == col).astype(jnp.float32)
    g = jnp.where(inside, g, eye)
    work = jnp.concatenate([g, eye, jnp.zeros((32, 64), jnp.float32)], 1)
    rows128 = lax.broadcasted_iota(jnp.int32, (32, LANES), 0)
    done = jnp.zeros((32, LANES), jnp.float32)
    for j in range(31):
        column = jnp.broadcast_to(work[:, j : j + 1], (32, LANES))
        pivot_row = jnp.broadcast_to(work[j : j + 1], (32, LANES))
        pivot = jnp.broadcast_to(column[j : j + 1], (32, LANES))
        done = jnp.where(rows128 == j, pivot_row / jnp.sqrt(pivot), done)
        work = work - column * (pivot_row / pivot)
    r = jnp.where((col >= row) & inside, done[:, :32], 0.0)
    l = jnp.where((col <= row) & inside, done[:, 32:64], 0.0)
    upper[...] = r
    lower[...] = l
    scaled = l * s
    hi = scaled.astype(jnp.bfloat16)
    lo = (scaled - hi.astype(jnp.float32)).astype(jnp.bfloat16)
    left = group_matrix((256, 32), 0, jnp.bfloat16)
    right = group_matrix((32, 256), 1, jnp.bfloat16)
    keep = same_layer()
    for part, out in ((hi, high), (lo, low)):
        wide = jnp.dot(left, part, preferred_element_type=jnp.float32)
        wide = jnp.dot(
            wide.astype(jnp.bfloat16), right, preferred_element_type=jnp.float32
        )
        out[...] = jnp.where(keep, wide, 0.0).astype(jnp.bfloat16)


def factor_call(gram, scale, weight):
    square = jax.ShapeDtypeStruct((256, 256), jnp.bfloat16)
    return call(
        functools.partial(factor_kernel, weight),
        (f32(32, 32), f32(32, 32), square, square),
        (gram, scale),
        in_specs=[WHOLE] * 2,
        out_specs=[WHOLE] * 4,
        flops=10**7,
        nbytes=10**6,
    )


def modes_kernel(basis, snaps, high, low, modes):
    for c in range(3):
        rows = merged_rows(basis, snaps, c)
        out = jnp.dot(high[...], rows, preferred_element_type=jnp.float32)
        out = out + jnp.dot(low[...], rows, preferred_element_type=jnp.float32)
        modes[:, c] = out.reshape(32, 8, out.shape[-1]).astype(jnp.bfloat16)


def modes_call(basis, snaps, high, low, width=1024):
    length = basis.shape[-1]
    whole = pl.BlockSpec((256, 256), lambda i: (0, 0))
    return call(
        modes_kernel,
        jax.ShapeDtypeStruct((32, 3, 8, length), jnp.bfloat16),
        (basis, snaps, high, low),
        grid=(length // width,),
        in_specs=column_specs(width) + [whole, whole],
        out_specs=pl.BlockSpec((32, 3, 8, width), lambda i: (0, 0, 0, i)),
        flops=4 * 256 * 256 * 3 * length,
        nbytes=63 * 3 * 8 * length * 2,
    )


def cross_kernel(basis, snaps, newest, cross, total):
    step = pl.program_id(0)
    width = newest.shape[-1]

    @pl.when(step == 0)
    def _():
        total[...] = jnp.zeros_like(total)

    new = [newest[c] for c in range(3)]

    def add(k, value):
        folded = sum(
            value[:, i * LANES : (i + 1) * LANES] for i in range(width // LANES)
        )
        total[k] += folded

    for k in range(31):
        ref, i = (basis, k) if k < 16 else (snaps, k - 16)
        add(k, sum(ref[i, c].astype(jnp.float32) * new[c] for c in range(3)))
    add(31, sum(n * n for n in new))

    @pl.when(step == pl.num_programs(0) - 1)
    def _():
        sums = jnp.sum(total[...], axis=1)
        line = lax.dot_general(
            jnp.ones((8, LANES), jnp.float32),
            sums,
            (((1,), (1,)), ((), ())),
            precision=lax.Precision.HIGHEST,
        )
        line = jnp.concatenate([line, jnp.zeros((8, 96), jnp.float32)], 1)
        cross[...] = jnp.broadcast_to(line[:1], cross.shape)


def cross_call(basis, snaps, newest, copies, width=512):
    length = basis.shape[-1]
    return call(
        cross_kernel,
        f32(copies, LANES),
        (basis, snaps, newest),
        [pltpu.VMEM((32, 8, LANES), jnp.float32)],
        grid=(length // width,),
        in_specs=column_specs(width) + [pl.BlockSpec((3, 8, width), lambda i: (0, 0, i))],
        out_specs=pl.BlockSpec((copies, LANES), lambda i: (0, 0)),
        flops=31 * 6 * 8 * length,
        nbytes=31 * 3 * 8 * length * 2,
    )


def last_kernel(
    weight, parts, scale, upper, lower, basis, snaps, newest, held, modes, factor, coef
):
    @pl.when(pl.program_id(0) == 0)
    def _():
        row = lax.broadcasted_iota(jnp.int32, (32, 32), 0)
        col = lax.broadcasted_iota(jnp.int32, (32, 32), 1)
        line = jnp.sum(parts[...], axis=0, keepdims=True)[:, :32]
        line = line * (weight * scale[...])
        l = lower[...]
        r = jnp.sum(l * line, axis=1, keepdims=True)
        rest = line[:, 31:32] - jnp.sum(r * r, axis=0, keepdims=True)
        diagonal = jnp.sqrt(rest)
        last = jnp.where(row < 31, r, diagonal)
        factor[...] = jnp.where(col == 31, last, upper[...])
        w = -jnp.sum(r * l, axis=0, keepdims=True) * scale[...] / diagonal
        w = jnp.where(col[:1] == 31, 1.0 / diagonal, w)
        for k in range(32):
            coef[k] = jnp.broadcast_to(w[:, k : k + 1], (8, LANES))

    width = newest.shape[-1]
    for i in range(width // LANES):
        at = slice(i * LANES, (i + 1) * LANES)
        totals = [coef[31] * newest[c, :, at] for c in range(3)]
        for k in range(31):
            ref, n = (basis, k) if k < 16 else (snaps, k - 16)
            for c in range(3):
                totals[c] = totals[c] + coef[k] * ref[n, c, :, at].astype(jnp.float32)
        for c in range(3):
            modes[0, c, :, at] = totals[c].astype(jnp.bfloat16)


def last_call(parts, scale, upper, lower, basis, snaps, newest, modes, weight, width=512):
    length = basis.shape[-1]
    small = pl.BlockSpec((32, 32), lambda i: (0, 0))
    return call(
        functools.partial(last_kernel, weight),
        (jax.ShapeDtypeStruct(modes.shape, modes.dtype), f32(32, 32)),
        (parts, scale, upper, lower, basis, snaps, newest, modes),
        [pltpu.VMEM((32, 8, LANES), jnp.float32)],
        grid=(length // width,),
        in_specs=[
            pl.BlockSpec(parts.shape, lambda i: (0, 0)),
            pl.BlockSpec((1, 32), lambda i: (0, 0)),
            small,
            small,
        ]
        + column_specs(width)
        + [
            pl.BlockSpec((3, 8, width), lambda i: (0, 0, i)),
            pl.BlockSpec(memory_space=pl.ANY),
        ],
        out_specs=[pl.BlockSpec((1, 3, 8, width), lambda i: (31, 0, 0, i)), small],
        input_output_aliases={7: 0},
        flops=31 * 6 * 8 * length,
        nbytes=31 * 3 * 8 * length * 2,
    )


def shifted(block, axis, distance):
    count = lax.axis_size(axis)
    route = [(i, (i + distance) % count) for i in range(count)]
    return lax.ppermute(block, axis, route)


def exchange(sends):
    to_below, to_above, first_y, last_y = sends
    above = shifted(to_below, "gx", -1)
    below = shifted(to_above, "gx", 1)
    before = shifted(last_y, "gy", 1)
    after = shifted(first_y, "gy", -1)
    return (above, below, before, after)


def summed(block, axis):
    count = lax.axis_size(axis)
    distance = 1
    while distance < count:
        route = [(i, i ^ distance) for i in range(count)]
        block = block + lax.ppermute(block, axis, route)
        distance *= 2
    return block


def local(density, momentum, energy, basis, scales, snapshots):
    rows, length = density.shape
    devices = lax.axis_size("gx") * lax.axis_size("gy")
    weight = 1.0 / (3 * rows * length * devices)
    fields = (density, momentum, energy)
    scale = jnp.concatenate([scales, jnp.ones((16,), jnp.float32)])[None]

    halo = exchange(pack(fields))
    gram = gram_call(basis, snapshots)
    first = stage_call(0, fields, None, halo)
    gram = summed(summed(gram, "gx"), "gy")
    halo = exchange(first[3:])
    second = stage_call(1, first[:3], fields, halo)
    upper, lower, high, low = factor_call(gram, scale, weight)
    halo = exchange(second[3:])
    modes = modes_call(basis, snapshots, high, low)
    final = stage_call(2, second[:3], fields, halo)
    newest = final[3]
    cross = cross_call(basis, snapshots, newest, devices)
    parts = lax.all_to_all(cross, ("gx", "gy"), 0, 0, tiled=True)
    modes, factor = last_call(
        parts, scale, upper, lower, basis, snapshots, newest, modes, weight
    )
    return (final[0], final[1], final[2], modes, factor)


def solution(mesh):
    field, vector = P("gx", "gy"), P(None, "gx", "gy")
    columns = P(None, None, "gx", "gy")
    return jax.shard_map(
        local,
        mesh=mesh,
        in_specs=(field, vector, field, columns, P(), columns),
        out_specs=(field, vector, field, columns, P()),
        check_vma=False,
    )
```

```python
import functools

import jax
import jax.numpy as jnp
import ml_dtypes
import numpy as np
from jax import lax
from jax.experimental import pallas as pl
from jax.experimental.pallas import tpu as pltpu
from jax.sharding import PartitionSpec as P

NZ = 64
LANES = 128
STEP_TIME = 0.03
FIRST = (0.8, -0.2, 4.0 / 105.0, -1.0 / 280.0)
SECOND = (8.0 / 5.0, -0.2, 8.0 / 315.0, -1.0 / 560.0)
CENTRAL = -205.0 / 72.0
UNROLL = (16, 16, 35, 16, 2)
VMEM_LIMIT = 48 * 1024 * 1024
WHOLE = pl.BlockSpec(memory_space=pltpu.VMEM)


def lanes_at(index):
    return pl.ds(pl.multiple_of(index * LANES, LANES), LANES)


def loop(count, body, unroll=1):
    def group(i, carry):
        for n in range(unroll):
            body(i * unroll + n)
        return carry

    lax.fori_loop(0, count // unroll, group, 0)
    for n in range(count - count % unroll, count):
        body(n)


def row_ids():
    return lax.broadcasted_iota(jnp.int32, (8, LANES), 0)


def lane_ids():
    return lax.broadcasted_iota(jnp.int32, (8, LANES), 1)


def primitives(rho, mx, my, mz, energy):
    inv = 1.0 / rho
    u, v, w = mx * inv, my * inv, mz * inv
    p = 0.4 * (energy - 0.5 * (mx * u + my * v + mz * w))
    return u, v, w, p, p * inv


def pack_sends(state, to_below, to_above, first_y, last_y):
    length = state[0].shape[-1]
    half = length // (2 * LANES)
    low = row_ids() < 4

    def body(j):
        for f in range(5):
            here = state[f][:, lanes_at(j)]
            other = pltpu.roll(state[f][:, lanes_at(j + half)], 4, 0)
            to_below[f, :, lanes_at(j)] = jnp.where(low, here, other)
            to_above[f, :, lanes_at(j)] = jnp.where(low, other, here)

    loop(half, body, UNROLL[0])
    width = 4 * NZ
    for f in range(5):
        first_y[f] = state[f][:, :width]
        last_y[f] = state[f][:, length - width :]


def state_views(rho, mom, energy):
    return [rho, mom.at[0], mom.at[1], mom.at[2], energy]


def pack_kernel(rho, mom, energy, to_below, to_above, first_y, last_y):
    pack_sends(state_views(rho, mom, energy), to_below, to_above, first_y, last_y)


def depth_weights():
    position = np.arange(LANES)
    same = position[:, None] // NZ == position[None, :] // NZ
    result = []
    for sign, coefficients in ((-1.0, FIRST), (1.0, SECOND)):
        full = np.zeros((LANES, LANES), np.float32)
        for k in range(1, 5):
            ahead = (position[None, :] + k - position[:, None]) % NZ == 0
            behind = (position[None, :] - k - position[:, None]) % NZ == 0
            full += coefficients[k - 1] * (same & ahead)
            full += sign * coefficients[k - 1] * (same & behind)
        hi = full.astype(ml_dtypes.bfloat16)
        lo = (full - hi.astype(np.float32)).astype(ml_dtypes.bfloat16)
        result.append(np.block([[hi, lo], [hi, np.zeros_like(lo)]]))
    return jnp.asarray(np.stack(result))


def stage_kernel(stage, refs):
    if stage == 0:
        rho, mom, energy, above, below, before, after, along_z = refs[:8]
        base = None
        rest = refs[8:]
    else:
        rho, mom, energy, rho0, mom0, energy0 = refs[:6]
        above, below, before, after, along_z = refs[6:11]
        base = state_views(rho0, mom0, energy0)
        rest = refs[11:]
    if stage < 2:
        rho_o, mom_o, energy_o, to_below, to_above, first_y, last_y = rest[:7]
        ys, yh, hx, zs, zd = rest[7:]
    else:
        rho_o, mom_o, energy_o, newest = rest[:4]
        ys, yh, hx, zs, zd = rest[4:]
    state = state_views(rho, mom, energy)
    outs = state_views(rho_o, mom_o, energy_o)
    length = rho.shape[-1]
    blocks = length // LANES
    half = blocks // 2
    row, lane = row_ids(), lane_ids()
    low = row < 4

    def fill(fields, at):
        r, mx, my, mz, e = fields
        u, v, w, p, t = primitives(r, mx, my, mz, e)
        for f, value in enumerate(
            (my, mx * v, my * v + p, mz * v, (e + p) * v, u, v, w, t, p)
        ):
            ys[f, :, at] = value
        return (mz, mx * w, my * w, mz * w + p, (e + p) * w, u, v, w, t)

    def fill_own(j):
        both = pl.ds(pl.multiple_of(j * 2 * LANES, 2 * LANES), 2 * LANES)
        at = pl.ds(pl.multiple_of(j * 2 * LANES + 2 * LANES, 2 * LANES), 2 * LANES)
        place = pl.ds(pl.multiple_of(j * 16, 16), 16)
        for f, value in enumerate(fill([s[:, both] for s in state], at)):
            tall = jnp.concatenate([value[:, :LANES], value[:, LANES:]], 0)
            hi = tall.astype(jnp.bfloat16)
            zs[f, place, :LANES] = hi
            zs[f, place, LANES:] = (tall - hi.astype(jnp.float32)).astype(jnp.bfloat16)

    loop(blocks // 2, fill_own, UNROLL[1])
    for f in range(9):
        wide = jnp.dot(
            zs[f], along_z[0 if f < 5 else 1], preferred_element_type=jnp.float32
        )
        zd[f] = wide[:, :LANES] + wide[:, LANES:]
    edge = 2 * LANES
    fill([before[f] for f in range(5)], slice(0, edge))
    fill([after[f] for f in range(5)], slice(length + edge, length + 2 * edge))

    def shift_half(j):
        for f in range(9):
            here, following = ys[f, :, lanes_at(j)], ys[f, :, lanes_at(j + 1)]
            yh[f, :, lanes_at(j)] = pltpu.roll(
                jnp.where(lane < NZ, following, here), NZ, 1
            )

    loop(blocks + 3, shift_half, UNROLL[2])

    def unpack(j):
        for f in range(5):
            a, b = above[f, :, lanes_at(j)], below[f, :, lanes_at(j)]
            hx[f, :, lanes_at(j)] = jnp.where(low, a, b)
            hx[f, :, lanes_at(j + half)] = pltpu.roll(jnp.where(low, b, a), 4, 0)

    loop(half, unpack, UNROLL[3])

    def main(j):
        at = lanes_at(j)
        own = [s[:, at] for s in state]
        r, mx, my, mz, e = own
        u, v, w, t, p = [ys[5 + f, :, lanes_at(j + 2)] for f in range(5)]
        energy_p = e + p
        hr, hmx, hmy, hmz, he = [hx[f, :, at] for f in range(5)]
        hu, hv, hw, hp, ht = primitives(hr, hmx, hmy, hmz, he)
        fx = (mx, mx * u + p, my * u, mz * u, energy_p * u, u, v, w, t)
        hfx = (hmx, hmx * hu + hp, hmy * hu, hmz * hu, (he + hp) * hu, hu, hv, hw, ht)
        here = pl.ds(pl.multiple_of(j * 8, 8), 8)
        result = []
        for f in range(9):
            total = zd[f, here, :]
            if f >= 5:
                total = total + (3.0 * CENTRAL) * fx[f]
            for k in range(1, 5):
                pairs = [
                    (
                        pltpu.roll(jnp.where(row < k, hfx[f], fx[f]), 8 - k, 0),
                        pltpu.roll(jnp.where(row >= 8 - k, hfx[f], fx[f]), k, 0),
                    ),
                ]
                if k % 2:
                    up, down = (k - 1) // 2, -(k + 1) // 2
                    pairs.append(
                        (yh[f, :, lanes_at(j + 2 + up)], yh[f, :, lanes_at(j + 2 + down)])
                    )
                else:
                    pairs.append(
                        (
                            ys[f, :, lanes_at(j + 2 + k // 2)],
                            ys[f, :, lanes_at(j + 2 - k // 2)],
                        )
                    )
                if f < 5:
                    s = sum(a - b for a, b in pairs)
                    term = FIRST[k - 1] * s
                else:
                    s = sum(a + b for a, b in pairs)
                    term = SECOND[k - 1] * s
                total = total + term
            result.append(total)
        visc = 0.08 * t
        lap = result[5:]
        work = visc * (u * lap[0] + v * lap[1] + w * lap[2] + 4.9 * lap[3])
        rate = [
            -result[0],
            visc * lap[0] - result[1],
            visc * lap[1] - result[2],
            visc * lap[2] - result[3],
            work - result[4],
        ]
        final = []
        for f in range(5):
            step = own[f] + STEP_TIME * rate[f]
            if stage == 1:
                step = 0.75 * base[f][:, at] + 0.25 * step
            elif stage == 2:
                step = base[f][:, at] * (1.0 / 3.0) + (2.0 / 3.0) * step
            outs[f][:, at] = step
            final.append(step)
        if stage == 2:
            inv = 1.0 / final[0]
            for c in range(3):
                newest[c, :, at] = final[1 + c] * inv

    loop(blocks, main, UNROLL[4])
    if stage < 2:
        pack_sends(outs, to_below, to_above, first_y, last_y)


def f32(*shape):
    return jax.ShapeDtypeStruct(shape, jnp.float32)


def call(kernel, out_shape, args, scratch=(), flops=0, nbytes=0, **kw):
    return pl.pallas_call(
        kernel,
        out_shape=out_shape,
        scratch_shapes=list(scratch),
        compiler_params=pltpu.CompilerParams(vmem_limit_bytes=VMEM_LIMIT),
        cost_estimate=pl.CostEstimate(
            flops=flops, bytes_accessed=nbytes, transcendentals=0
        ),
        **kw,
    )(*args)


def state_shapes(rows, length):
    return (f32(rows, length), f32(3, rows, length), f32(rows, length))


def send_shapes(rows, length):
    packed = f32(5, rows, length // 2)
    edge = f32(5, rows, 4 * NZ)
    return (packed, packed, edge, edge)


def pack(state):
    rows, length = state[0].shape
    shapes = send_shapes(rows, length)
    return call(
        pack_kernel,
        shapes,
        state,
        in_specs=[WHOLE] * 3,
        out_specs=[WHOLE] * 4,
        nbytes=10**6,
    )


def stage_call(stage, state, base, halo):
    rows, length = state[0].shape
    out = state_shapes(rows, length)
    out += send_shapes(rows, length) if stage < 2 else (f32(3, rows, length),)
    args = tuple(state) + (tuple(base) if stage else ()) + tuple(halo) + (depth_weights(),)
    scratch = [
        pltpu.VMEM((10, rows, length + 8 * NZ), jnp.float32),
        pltpu.VMEM((9, rows, length + 8 * NZ), jnp.float32),
        pltpu.VMEM((5, rows, length), jnp.float32),
        pltpu.VMEM((9, length // 16, 2 * LANES), jnp.bfloat16),
        pltpu.VMEM((9, length // 16, LANES), jnp.float32),
    ]
    return call(
        lambda *refs: stage_kernel(stage, refs),
        out,
        args,
        scratch,
        in_specs=[WHOLE] * len(args),
        out_specs=[WHOLE] * len(out),
        flops=32768 * 700,
        nbytes=3 * 10**6,
    )


def merged_rows(basis, snaps, c, at):
    first = basis[:, c, :, at].astype(jnp.float32)
    second = snaps[:, c, :, at].astype(jnp.float32)
    length = first.shape[-1]
    rows = jnp.concatenate([first, second, jnp.zeros((1, 8, length), jnp.float32)], 0)
    return rows.reshape(256, length).astype(jnp.bfloat16)


def group_matrix(shape, group_dim, dtype):
    g = lax.broadcasted_iota(jnp.int32, shape, group_dim)
    o = lax.broadcasted_iota(jnp.int32, shape, 1 - group_dim)
    return (g // 8 == o).astype(dtype)


def same_layer():
    r = lax.broadcasted_iota(jnp.int32, (256, 256), 0)
    c = lax.broadcasted_iota(jnp.int32, (256, 256), 1)
    return r % 8 == c % 8


def pack_square(small):
    return jnp.concatenate([small[8 * g : 8 * g + 8] for g in range(4)], 1)


def gram_kernel(basis, snaps, gram, total):
    width = 1024
    total[...] = jnp.zeros_like(total)

    def add(i):
        at = pl.ds(pl.multiple_of(i * width, width), width)
        for c in range(3):
            rows = merged_rows(basis, snaps, c, at)
            total[...] += lax.dot_general(
                rows, rows, (((1,), (1,)), ((), ())), preferred_element_type=jnp.float32
            )

    loop(basis.shape[-1] // width, add)
    kept = jnp.where(same_layer(), total[...], 0.0)
    left = group_matrix((32, 256), 1, jnp.float32)
    right = group_matrix((256, 32), 0, jnp.float32)
    small = jnp.dot(left, kept, precision=lax.Precision.HIGHEST)
    gram[...] = pack_square(jnp.dot(small, right, precision=lax.Precision.HIGHEST))


def gram_call(basis, snaps):
    length = basis.shape[-1]
    return call(
        gram_kernel,
        f32(8, LANES),
        (basis, snaps),
        [pltpu.VMEM((256, 256), jnp.float32)],
        in_specs=[WHOLE] * 2,
        out_specs=WHOLE,
        flops=2 * 256 * 256 * 3 * length,
        nbytes=31 * 3 * 8 * length * 2,
    )


def cross_kernel(basis, snaps, newest, gram, parts, total):
    total[...] = jnp.zeros_like(total)

    def add(i):
        at = lanes_at(i)
        new = [newest[c, :, at] for c in range(3)]
        for k in range(31):
            ref, n = (basis, k) if k < 16 else (snaps, k - 16)
            total[k] += sum(ref[n, c, :, at].astype(jnp.float32) * new[c] for c in range(3))
        total[31] += sum(n * n for n in new)

    loop(basis.shape[-1] // LANES, add, 4)
    sums = jnp.sum(total[...], axis=1)
    line = lax.dot_general(
        jnp.ones((8, LANES), jnp.float32),
        sums,
        (((1,), (1,)), ((), ())),
        precision=lax.Precision.HIGHEST,
    )
    line = jnp.concatenate([jnp.zeros((8, 96), jnp.float32), line], 1)
    last = (row_ids() == 7) & (lane_ids() >= 96)
    parts[...] = jnp.broadcast_to(jnp.where(last, line, gram[...])[None], parts.shape)


def cross_call(basis, snaps, newest, gram, copies):
    length = basis.shape[-1]
    return call(
        cross_kernel,
        f32(copies, 8, LANES),
        (basis, snaps, newest, gram),
        [pltpu.VMEM((32, 8, LANES), jnp.float32)],
        in_specs=[WHOLE] * 4,
        out_specs=WHOLE,
        flops=31 * 6 * 8 * length,
        nbytes=31 * 3 * 8 * length * 2,
    )


def weights_of(weight, parts, scale, factor, high, low, diagonal):
    row = lax.broadcasted_iota(jnp.int32, (32, 32), 0)
    col = lax.broadcasted_iota(jnp.int32, (32, 32), 1)
    s = jnp.broadcast_to(scale[...], (32, 32))
    s_col = jnp.sum(jnp.where(row == col, s, 0.0), axis=1, keepdims=True)
    packed = jnp.sum(parts[...], axis=0)
    g = jnp.concatenate([packed[:, 32 * i : 32 * i + 32] for i in range(4)], 0)
    line = jnp.broadcast_to(g[31:32], (32, 32))
    line = jnp.sum(jnp.where(row == col, line, 0.0), axis=1, keepdims=True)
    g = jnp.where(col == 31, line, g)
    g = g * (weight * s) * s_col
    eye = (row == col).astype(jnp.float32)
    work = jnp.concatenate([g, eye, jnp.zeros((32, 64), jnp.float32)], 1)
    rows128 = lax.broadcasted_iota(jnp.int32, (32, LANES), 0)
    done = jnp.zeros((32, LANES), jnp.float32)
    for j in range(32):
        column = jnp.broadcast_to(work[:, j : j + 1], (32, LANES))
        pivot_row = jnp.broadcast_to(work[j : j + 1], (32, LANES))
        pivot = jnp.broadcast_to(column[j : j + 1], (32, LANES))
        done = jnp.where(rows128 == j, pivot_row / jnp.sqrt(pivot), done)
        work = work - column * (pivot_row / pivot)
    factor[...] = jnp.where(col >= row, done[:, :32], 0.0)
    l = jnp.where(col <= row, done[:, 32:64], 0.0)
    diagonal[...] = jnp.broadcast_to(l[31:32, 31:32], diagonal.shape)
    scaled = jnp.where(col < 31, l * s, 0.0)
    hi = scaled.astype(jnp.bfloat16)
    lo = (scaled - hi.astype(jnp.float32)).astype(jnp.bfloat16)
    left = group_matrix((256, 32), 0, jnp.bfloat16)
    right = group_matrix((32, 256), 1, jnp.bfloat16)
    keep = same_layer()
    for part, out in ((hi, high), (lo, low)):
        wide = jnp.dot(left, part, preferred_element_type=jnp.float32)
        wide = jnp.dot(
            wide.astype(jnp.bfloat16), right, preferred_element_type=jnp.float32
        )
        out[...] = jnp.where(keep, wide, 0.0).astype(jnp.bfloat16)


def modes_kernel(
    weight, parts, scale, basis, snaps, newest, modes, factor, high, low, diagonal
):
    step = pl.program_id(0)

    @pl.when(step == 0)
    def _():
        weights_of(weight, parts, scale, factor, high, low, diagonal)

    width = modes.shape[-1]
    at = pl.ds(pl.multiple_of(step * width, width), width)
    for c in range(3):
        rows = merged_rows(basis, snaps, c, at)
        out = jnp.dot(high[...], rows, preferred_element_type=jnp.float32)
        out = out + jnp.dot(low[...], rows, preferred_element_type=jnp.float32)
        out = out.reshape(32, 8, width)
        modes[:31, c] = out[:31].astype(jnp.bfloat16)
        own = diagonal[:, :1] * newest[c, :, at]
        modes[31, c] = (out[31] + own).astype(jnp.bfloat16)


def modes_call(parts, scale, basis, snaps, newest, weight, width=1024):
    length = basis.shape[-1]
    return call(
        functools.partial(modes_kernel, weight),
        (jax.ShapeDtypeStruct((32, 3, 8, length), jnp.bfloat16), f32(32, 32)),
        (parts, scale, basis, snaps, newest),
        [
            pltpu.VMEM((256, 256), jnp.bfloat16),
            pltpu.VMEM((256, 256), jnp.bfloat16),
            pltpu.VMEM((8, LANES), jnp.float32),
        ],
        grid=(length // width,),
        in_specs=[WHOLE] * 5,
        out_specs=[
            pl.BlockSpec((32, 3, 8, width), lambda i: (0, 0, 0, i)),
            pl.BlockSpec((32, 32), lambda i: (0, 0)),
        ],
        flops=4 * 256 * 256 * 3 * length,
        nbytes=63 * 3 * 8 * length * 2,
    )


def shifted(block, axis, distance):
    count = lax.axis_size(axis)
    route = [(i, (i + distance) % count) for i in range(count)]
    return lax.ppermute(block, axis, route)


def exchange(sends):
    to_below, to_above, first_y, last_y = sends
    above = shifted(to_below, "gx", -1)
    below = shifted(to_above, "gx", 1)
    before = shifted(last_y, "gy", 1)
    after = shifted(first_y, "gy", -1)
    return (above, below, before, after)


def local(density, momentum, energy, basis, scales, snapshots):
    rows, length = density.shape
    devices = lax.axis_size("gx") * lax.axis_size("gy")
    weight = 1.0 / (3 * rows * length * devices)
    fields = (density, momentum, energy)
    scale = jnp.concatenate([scales, jnp.ones((16,), jnp.float32)])[None]

    halo = exchange(pack(fields))
    gram = gram_call(basis, snapshots)
    first = stage_call(0, fields, None, halo)
    second = stage_call(1, first[:3], fields, exchange(first[3:]))
    final = stage_call(2, second[:3], fields, exchange(second[3:]))
    newest = final[3]
    parts = cross_call(basis, snapshots, newest, gram, devices)
    parts = lax.all_to_all(parts, ("gx", "gy"), 0, 0, tiled=True)
    modes, factor = modes_call(parts, scale, basis, snapshots, newest, weight)
    return (final[0], final[1], final[2], modes, factor)


def solution(mesh):
    field, vector = P("gx", "gy"), P(None, "gx", "gy")
    columns = P(None, None, "gx", "gy")
    return jax.shard_map(
        local,
        mesh=mesh,
        in_specs=(field, vector, field, columns, P(), columns),
        out_specs=(field, vector, field, columns, P()),
        check_vma=False,
    )
```

```python
import functools

import jax
import jax.numpy as jnp
import ml_dtypes
import numpy as np
from jax import lax
from jax.experimental import pallas as pl
from jax.experimental.pallas import tpu as pltpu
from jax.sharding import PartitionSpec as P

NZ = 64
LANES = 128
STEP_TIME = 0.03
FIRST = (0.8, -0.2, 4.0 / 105.0, -1.0 / 280.0)
SECOND = (8.0 / 5.0, -0.2, 8.0 / 315.0, -1.0 / 560.0)
CENTRAL = -205.0 / 72.0
UNROLL = (16, 16, 35, 16, 2)
VMEM_LIMIT = 20 * 1024 * 1024
WHOLE = pl.BlockSpec(memory_space=pltpu.VMEM)
SCALAR = pl.BlockSpec(memory_space=pltpu.SMEM)


def lanes_at(index):
    return pl.ds(pl.multiple_of(index * LANES, LANES), LANES)


def loop(count, body, unroll=1):
    def group(i, carry):
        for n in range(unroll):
            body(i * unroll + n)
        return carry

    lax.fori_loop(0, count // unroll, group, 0)
    for n in range(count - count % unroll, count):
        body(n)


def row_ids():
    return lax.broadcasted_iota(jnp.int32, (8, LANES), 0)


def lane_ids():
    return lax.broadcasted_iota(jnp.int32, (8, LANES), 1)


def primitives(rho, mx, my, mz, energy):
    inv = 1.0 / rho
    u, v, w = mx * inv, my * inv, mz * inv
    p = 0.4 * (energy - 0.5 * (mx * u + my * v + mz * w))
    return u, v, w, p, p * inv


def low_rows(odd):
    return (row_ids() ^ (4 * odd[0])) < 4


def pack_sends(state, odd, to_far, to_near, first_y, last_y):
    length = state[0].shape[-1]
    half = length // (2 * LANES)
    low = low_rows(odd)

    def body(j):
        for f in range(5):
            here = state[f][:, lanes_at(j)]
            other = pltpu.roll(state[f][:, lanes_at(j + half)], 4, 0)
            to_far[f, :, lanes_at(j)] = jnp.where(low, here, other)
            to_near[f, :, lanes_at(j)] = jnp.where(low, other, here)

    loop(half, body, UNROLL[0])
    width = 4 * NZ
    for f in range(5):
        first_y[f] = state[f][:, :width]
        last_y[f] = state[f][:, length - width :]


def state_views(rho, mom, energy):
    return [rho, mom.at[0], mom.at[1], mom.at[2], energy]


def pack_kernel(odd, rho_h, mom_h, energy_h, z_h, rho, mom, energy, along_z, *rest):
    *sends, sems = rest
    pairs = ((rho_h, rho), (mom_h, mom), (energy_h, energy), (z_h, along_z))
    copies = [pltpu.make_async_copy(a, b, sems.at[i]) for i, (a, b) in enumerate(pairs)]
    for copy in copies:
        copy.start()
    for copy in copies:
        copy.wait()
    pack_sends(state_views(rho, mom, energy), odd, *sends)


def depth_weights():
    position = np.arange(LANES)
    same = position[:, None] // NZ == position[None, :] // NZ
    result = []
    for sign, coefficients in ((-1.0, FIRST), (1.0, SECOND)):
        full = np.zeros((LANES, LANES), np.float32)
        for k in range(1, 5):
            ahead = (position[None, :] + k - position[:, None]) % NZ == 0
            behind = (position[None, :] - k - position[:, None]) % NZ == 0
            full += coefficients[k - 1] * (same & ahead)
            full += sign * coefficients[k - 1] * (same & behind)
        hi = full.astype(ml_dtypes.bfloat16)
        lo = (full - hi.astype(np.float32)).astype(ml_dtypes.bfloat16)
        result.append(np.block([[hi, lo], [hi, np.zeros_like(lo)]]))
    return jnp.asarray(np.stack(result))


def stage_kernel(stage, refs):
    odd, along_z, far, near, before, after, rho, mom, energy = refs[:9]
    base = state_views(*refs[9:12]) if stage else None
    rest = refs[12:] if stage else refs[9:]
    if stage < 2:
        rho_o, mom_o, energy_o = rest[:3]
        sends = rest[3:7]
        ys, yh, hx, zs, zd = rest[7:]
    else:
        rho_o, mom_o, energy_o, newest = rest[:4]
        ys, yh, hx, zs, zd = rest[4:]
    state = state_views(rho, mom, energy)
    outs = state_views(rho_o, mom_o, energy_o)
    length = rho.shape[-1]
    blocks = length // LANES
    half = blocks // 2
    row, lane = row_ids(), lane_ids()
    low = low_rows(odd)

    def fill(fields, at):
        r, mx, my, mz, e = fields
        u, v, w, p, t = primitives(r, mx, my, mz, e)
        for f, value in enumerate(
            (my, mx * v, my * v + p, mz * v, (e + p) * v, u, v, w, t, p)
        ):
            ys[f, :, at] = value
        return (mz, mx * w, my * w, mz * w + p, (e + p) * w, u, v, w, t)

    def fill_own(j):
        both = pl.ds(pl.multiple_of(j * 2 * LANES, 2 * LANES), 2 * LANES)
        at = pl.ds(pl.multiple_of(j * 2 * LANES + 2 * LANES, 2 * LANES), 2 * LANES)
        place = pl.ds(pl.multiple_of(j * 16, 16), 16)
        for f, value in enumerate(fill([s[:, both] for s in state], at)):
            tall = jnp.concatenate([value[:, :LANES], value[:, LANES:]], 0)
            hi = tall.astype(jnp.bfloat16)
            zs[f, place, :LANES] = hi
            zs[f, place, LANES:] = (tall - hi.astype(jnp.float32)).astype(jnp.bfloat16)

    loop(blocks // 2, fill_own, UNROLL[1])
    for f in range(9):
        wide = jnp.dot(
            zs[f], along_z[0 if f < 5 else 1], preferred_element_type=jnp.float32
        )
        zd[f] = wide[:, :LANES] + wide[:, LANES:]
    edge = 2 * LANES
    fill([before[f] for f in range(5)], slice(0, edge))
    fill([after[f] for f in range(5)], slice(length + edge, length + 2 * edge))

    def shift_half(j):
        for f in range(9):
            here, following = ys[f, :, lanes_at(j)], ys[f, :, lanes_at(j + 1)]
            yh[f, :, lanes_at(j)] = pltpu.roll(
                jnp.where(lane < NZ, following, here), NZ, 1
            )

    loop(blocks + 3, shift_half, UNROLL[2])

    def unpack(j):
        for f in range(5):
            a, b = near[f, :, lanes_at(j)], far[f, :, lanes_at(j)]
            hx[f, :, lanes_at(j)] = jnp.where(low, a, b)
            hx[f, :, lanes_at(j + half)] = pltpu.roll(jnp.where(low, b, a), 4, 0)

    loop(half, unpack, UNROLL[3])

    def main(j):
        at = lanes_at(j)
        own = [s[:, at] for s in state]
        r, mx, my, mz, e = own
        u, v, w, t, p = [ys[5 + f, :, lanes_at(j + 2)] for f in range(5)]
        energy_p = e + p
        hr, hmx, hmy, hmz, he = [hx[f, :, at] for f in range(5)]
        hu, hv, hw, hp, ht = primitives(hr, hmx, hmy, hmz, he)
        fx = (mx, mx * u + p, my * u, mz * u, energy_p * u, u, v, w, t)
        hfx = (hmx, hmx * hu + hp, hmy * hu, hmz * hu, (he + hp) * hu, hu, hv, hw, ht)
        here = pl.ds(pl.multiple_of(j * 8, 8), 8)
        result = []
        for f in range(9):
            total = zd[f, here, :]
            if f >= 5:
                total = total + (3.0 * CENTRAL) * fx[f]
            for k in range(1, 5):
                pairs = [
                    (
                        pltpu.roll(jnp.where(row < k, hfx[f], fx[f]), 8 - k, 0),
                        pltpu.roll(jnp.where(row >= 8 - k, hfx[f], fx[f]), k, 0),
                    ),
                ]
                if k % 2:
                    up, down = (k - 1) // 2, -(k + 1) // 2
                    pairs.append(
                        (yh[f, :, lanes_at(j + 2 + up)], yh[f, :, lanes_at(j + 2 + down)])
                    )
                else:
                    pairs.append(
                        (
                            ys[f, :, lanes_at(j + 2 + k // 2)],
                            ys[f, :, lanes_at(j + 2 - k // 2)],
                        )
                    )
                if f < 5:
                    s = sum(a - b for a, b in pairs)
                    term = FIRST[k - 1] * s
                else:
                    s = sum(a + b for a, b in pairs)
                    term = SECOND[k - 1] * s
                total = total + term
            result.append(total)
        visc = 0.08 * t
        lap = result[5:]
        work = visc * (u * lap[0] + v * lap[1] + w * lap[2] + 4.9 * lap[3])
        rate = [
            -result[0],
            visc * lap[0] - result[1],
            visc * lap[1] - result[2],
            visc * lap[2] - result[3],
            work - result[4],
        ]
        final = []
        for f in range(5):
            step = own[f] + STEP_TIME * rate[f]
            if stage == 1:
                step = 0.75 * base[f][:, at] + 0.25 * step
            elif stage == 2:
                step = base[f][:, at] * (1.0 / 3.0) + (2.0 / 3.0) * step
            outs[f][:, at] = step
            final.append(step)
        if stage == 2:
            inv = 1.0 / final[0]
            for c in range(3):
                newest[c, :, at] = final[1 + c] * inv

    loop(blocks, main, UNROLL[4])
    if stage < 2:
        pack_sends(outs, odd, *sends)


def f32(*shape):
    return jax.ShapeDtypeStruct(shape, jnp.float32)


def call(kernel, out_shape, args, scratch=(), flops=0, nbytes=0, vmem=VMEM_LIMIT, **kw):
    return pl.pallas_call(
        kernel,
        out_shape=out_shape,
        scratch_shapes=list(scratch),
        compiler_params=pltpu.CompilerParams(vmem_limit_bytes=vmem),
        cost_estimate=pl.CostEstimate(
            flops=flops, bytes_accessed=nbytes, transcendentals=0
        ),
        **kw,
    )(*args)


def in_hbm(*arrays):
    return tuple(pltpu.with_memory_space_constraint(a, pltpu.HBM) for a in arrays)


def state_shapes(rows, length):
    return (f32(rows, length), f32(3, rows, length), f32(rows, length))


def send_shapes(rows, length):
    packed = f32(5, rows, length // 2)
    edge = f32(5, rows, 4 * NZ)
    return (packed, packed, edge, edge)


def pack(odd, state):
    rows, length = state[0].shape
    weights = depth_weights()
    shapes = state_shapes(rows, length)
    shapes += (jax.ShapeDtypeStruct(weights.shape, weights.dtype),)
    shapes += send_shapes(rows, length)
    out = call(
        pack_kernel,
        shapes,
        (odd, *in_hbm(*state, weights)),
        [pltpu.SemaphoreType.DMA((4,))],
        in_specs=[SCALAR] + [pl.BlockSpec(memory_space=pltpu.HBM)] * 4,
        out_specs=[WHOLE] * 8,
        nbytes=10**6,
    )
    return out[:3], out[3], out[4:]


def stage_call(stage, odd, along_z, halo, state, base):
    rows, length = state[0].shape
    out = state_shapes(rows, length)
    out += send_shapes(rows, length) if stage < 2 else (f32(3, rows, length),)
    args = (odd, along_z, *halo, *state) + (tuple(base) if stage else ())
    scratch = [
        pltpu.VMEM((10, rows, length + 8 * NZ), jnp.float32),
        pltpu.VMEM((9, rows, length + 8 * NZ), jnp.float32),
        pltpu.VMEM((5, rows, length), jnp.float32),
        pltpu.VMEM((9, length // 16, 2 * LANES), jnp.bfloat16),
        pltpu.VMEM((9, length // 16, LANES), jnp.float32),
    ]
    return call(
        lambda *refs: stage_kernel(stage, refs),
        out,
        args,
        scratch,
        in_specs=[SCALAR] + [WHOLE] * (len(args) - 1),
        out_specs=[WHOLE] * len(out),
        flops=32768 * 700,
        nbytes=3 * 10**6,
    )


def merged_rows(basis, snaps, c, at):
    first = basis[:, c, :, at].astype(jnp.float32)
    second = snaps[:, c, :, at].astype(jnp.float32)
    length = first.shape[-1]
    rows = jnp.concatenate([first, second, jnp.zeros((1, 8, length), jnp.float32)], 0)
    return rows.reshape(256, length).astype(jnp.bfloat16)


def group_matrix(shape, group_dim, dtype):
    g = lax.broadcasted_iota(jnp.int32, shape, group_dim)
    o = lax.broadcasted_iota(jnp.int32, shape, 1 - group_dim)
    return (g // 8 == o).astype(dtype)


def same_layer():
    r = lax.broadcasted_iota(jnp.int32, (256, 256), 0)
    c = lax.broadcasted_iota(jnp.int32, (256, 256), 1)
    return r % 8 == c % 8


def pack_square(small):
    return jnp.concatenate([small[8 * g : 8 * g + 8] for g in range(4)], 1)


GRAM_WIDTH = 1024


def gram_kernel(basis_h, snaps_h, gram, merged, basis, snaps, total, sems):
    width = GRAM_WIDTH
    places = [slice(i, i + width) for i in range(0, basis_h.shape[-1], width)]
    loads = []
    for n, at in enumerate(places):
        for m, (source, held) in enumerate(((basis_h, basis), (snaps_h, snaps))):
            loads.append(
                pltpu.make_async_copy(
                    source.at[:, :, :, at], held.at[:, :, :, at], sems.at[n, m]
                )
            )
            loads[-1].start()
    total[...] = jnp.zeros_like(total)
    for n, at in enumerate(places):
        loads[2 * n].wait()
        loads[2 * n + 1].wait()
        for c in range(3):
            rows = merged_rows(basis, snaps, c, at)
            merged[c, :, at] = rows
            total[...] += lax.dot_general(
                rows, rows, (((1,), (1,)), ((), ())), preferred_element_type=jnp.float32
            )
    kept = jnp.where(same_layer(), total[...], 0.0)
    left = group_matrix((32, 256), 1, jnp.float32)
    right = group_matrix((256, 32), 0, jnp.float32)
    small = jnp.dot(left, kept, precision=lax.Precision.HIGHEST)
    small = jnp.dot(small, right, precision=lax.Precision.HIGHEST)
    gram[...] = pack_square(small)


def gram_call(basis, snaps):
    length = basis.shape[-1]
    hbm = pl.BlockSpec(memory_space=pltpu.HBM)
    return call(
        gram_kernel,
        (f32(8, LANES), pltpu.VMEM((3, 256, length), jnp.bfloat16)),
        in_hbm(basis, snaps),
        [
            pltpu.VMEM(basis.shape, jnp.bfloat16),
            pltpu.VMEM(snaps.shape, jnp.bfloat16),
            pltpu.VMEM((256, 256), jnp.float32),
            pltpu.SemaphoreType.DMA((length // GRAM_WIDTH, 2)),
        ],
        in_specs=[hbm, hbm],
        out_specs=[WHOLE] * 2,
        flops=2 * 256 * 256 * 3 * length,
        nbytes=31 * 3 * 8 * length * 2,
    )


def cross_kernel(merged, newest, gram, parts, total):
    blocks = newest.shape[-1] // LANES

    def add(i):
        pair = pl.ds(pl.multiple_of(i * 16, 16), 16)
        sums = [jnp.zeros((2, 8, LANES), jnp.float32) for _ in range(4)]
        for n in range(3 * blocks):
            c, at = n % 3, slice(n // 3 * LANES, (n // 3 + 1) * LANES)
            rows = merged[c, pair, at].astype(jnp.float32).reshape(2, 8, LANES)
            sums[n % 4] = sums[n % 4] + rows * newest[c, :, at]
        total[pl.ds(i * 2, 2)] = (sums[0] + sums[1]) + (sums[2] + sums[3])

    loop(16, add)
    own = [jnp.zeros((8, LANES), jnp.float32) for _ in range(4)]
    for n in range(3 * blocks):
        value = newest[n % 3, :, n // 3 * LANES : (n // 3 + 1) * LANES]
        own[n % 4] = own[n % 4] + value * value
    total[31] = (own[0] + own[1]) + (own[2] + own[3])
    sums = jnp.sum(total[...], axis=1)
    line = lax.dot_general(
        jnp.ones((8, LANES), jnp.float32),
        sums,
        (((1,), (1,)), ((), ())),
        precision=lax.Precision.HIGHEST,
    )
    line = jnp.concatenate([jnp.zeros((8, 96), jnp.float32), line], 1)
    last = (row_ids() == 7) & (lane_ids() >= 96)
    parts[...] = jnp.broadcast_to(jnp.where(last, line, gram[...])[None], parts.shape)


def cross_call(merged, newest, gram, copies):
    length = newest.shape[-1]
    return call(
        cross_kernel,
        f32(copies, 8, LANES),
        (merged, newest, gram),
        [pltpu.VMEM((32, 8, LANES), jnp.float32)],
        in_specs=[WHOLE] * 3,
        out_specs=WHOLE,
        flops=31 * 6 * 8 * length,
        nbytes=31 * 3 * 8 * length * 2,
    )


def eliminated(work):
    wide = (8, LANES)
    blocks = [work[8 * i : 8 * i + 8] for i in range(4)]
    row = row_ids()
    done = []
    for b in range(4):
        columns = [
            {i: jnp.broadcast_to(blocks[i][:, 8 * b + s : 8 * b + s + 1], wide) for i in range(b, 4)}
            for s in range(8)
        ]
        rows = [jnp.broadcast_to(blocks[b][s : s + 1], wide) for s in range(8)]
        result = jnp.zeros(wide, jnp.float32)
        scaled = []
        for t in range(8):
            pivot = jnp.broadcast_to(columns[t][b][t : t + 1], wide)
            inv = 1.0 / pivot
            result = jnp.where(row == t, rows[t] / jnp.sqrt(pivot), result)
            scaled.append(rows[t] * inv)
            for s in range(t + 1, 8):
                ratio = jnp.broadcast_to(columns[s][b][t : t + 1], wide) * inv
                below = jnp.broadcast_to(columns[t][b][s : s + 1], wide)
                rows[s] = rows[s] - below * scaled[t]
                for i in range(b, 4):
                    columns[s][i] = columns[s][i] - columns[t][i] * ratio
        done.append(result)
        for i in range(b + 1, 4):
            for t in range(8):
                blocks[i] = blocks[i] - columns[t][i] * scaled[t]
    return jnp.concatenate(done, 0)


def weights_of(weight, parts, scale, factor, high, low, diagonal):
    row = lax.broadcasted_iota(jnp.int32, (32, 32), 0)
    col = lax.broadcasted_iota(jnp.int32, (32, 32), 1)
    s = jnp.broadcast_to(scale[...], (32, 32))
    s_col = jnp.sum(jnp.where(row == col, s, 0.0), axis=1, keepdims=True)
    packed = jnp.sum(parts[...], axis=0)
    g = jnp.concatenate([packed[:, 32 * i : 32 * i + 32] for i in range(4)], 0)
    line = jnp.broadcast_to(g[31:32], (32, 32))
    line = jnp.sum(jnp.where(row == col, line, 0.0), axis=1, keepdims=True)
    g = jnp.where(col == 31, line, g)
    g = g * (weight * s) * s_col
    eye = (row == col).astype(jnp.float32)
    done = eliminated(jnp.concatenate([g, eye, jnp.zeros((32, 64), jnp.float32)], 1))
    factor[...] = jnp.where(col >= row, done[:, :32], 0.0)
    l = jnp.where(col <= row, done[:, 32:64], 0.0)
    diagonal[...] = jnp.broadcast_to(l[31:32, 31:32], diagonal.shape)
    scaled = jnp.where(col < 31, l * s, 0.0)
    hi = scaled.astype(jnp.bfloat16)
    lo = (scaled - hi.astype(jnp.float32)).astype(jnp.bfloat16)
    left = group_matrix((256, 32), 0, jnp.bfloat16)
    right = group_matrix((32, 256), 1, jnp.bfloat16)
    keep = same_layer()
    for part, out in ((hi, high), (lo, low)):
        wide = jnp.dot(left, part, preferred_element_type=jnp.float32)
        wide = jnp.dot(
            wide.astype(jnp.bfloat16), right, preferred_element_type=jnp.float32
        )
        out[...] = jnp.where(keep, wide, 0.0).astype(jnp.bfloat16)


MODES_WIDTH = 2048


def modes_kernel(
    weight,
    parts,
    scale,
    merged,
    newest,
    modes,
    factor,
    out,
    high,
    low,
    diagonal,
    out_sems,
):
    width = MODES_WIDTH
    pieces = []
    for i in range(newest.shape[-1] // width):
        for c in range(3):
            pieces.append((len(pieces), c, slice(i * width, (i + 1) * width)))
    weights_of(weight, parts, scale, factor, high, low, diagonal)
    stores = []
    for n, c, at in pieces:
        rows = merged[c, :, at]
        value = jnp.dot(high[...], rows, preferred_element_type=jnp.float32)
        value = value + jnp.dot(low[...], rows, preferred_element_type=jnp.float32)
        value = value.reshape(32, 8, width)
        out[:31, c, :, at] = value[:31].astype(jnp.bfloat16)
        own = diagonal[:, :1] * newest[c, :, at]
        out[31, c, :, at] = (value[31] + own).astype(jnp.bfloat16)
        store = pltpu.make_async_copy(
            out.at[:, c, :, at], modes.at[:, c, :, at], out_sems.at[n]
        )
        store.start()
        stores.append(store)
    for store in stores:
        store.wait()


def modes_call(parts, scale, merged, newest, weight):
    length = newest.shape[-1]
    count = 3 * length // MODES_WIDTH
    shape = (32, 3, 8, length)
    return call(
        functools.partial(modes_kernel, weight),
        (jax.ShapeDtypeStruct(shape, jnp.bfloat16), f32(32, 32)),
        (parts, scale, merged, newest),
        [
            pltpu.VMEM(shape, jnp.bfloat16),
            pltpu.VMEM((256, 256), jnp.bfloat16),
            pltpu.VMEM((256, 256), jnp.bfloat16),
            pltpu.VMEM((8, LANES), jnp.float32),
            pltpu.SemaphoreType.DMA((count,)),
        ],
        in_specs=[WHOLE] * 4,
        out_specs=[pl.BlockSpec(memory_space=pltpu.HBM), WHOLE],
        flops=4 * 256 * 256 * 3 * length,
        nbytes=63 * 3 * 8 * length * 2,
    )


def shifted(block, axis, distance):
    count = lax.axis_size(axis)
    route = [(i, (i + distance) % count) for i in range(count)]
    return lax.ppermute(block, axis, route)


def exchange(sends):
    to_far, to_near, first_y, last_y = sends
    count = lax.axis_size("gx")
    pairs = [(i, (i + 1) % count) for i in range(1, count, 2)]
    far = lax.ppermute(to_far, "gx", pairs + [(j, i) for i, j in pairs])
    near = lax.ppermute(to_near, "gx", [(i, i ^ 1) for i in range(count)])
    before = shifted(last_y, "gy", 1)
    after = shifted(first_y, "gy", -1)
    return (far, near, before, after)


def local(density, momentum, energy, basis, scales, snapshots):
    rows, length = density.shape
    devices = lax.axis_size("gx") * lax.axis_size("gy")
    weight = 1.0 / (3 * rows * length * devices)
    fields = (density, momentum, energy)
    scale = jnp.concatenate([scales, jnp.ones((16,), jnp.float32)])[None]

    odd = (lax.axis_index("gx") % 2).astype(jnp.int32)[None]
    fields, along_z, sends = pack(odd, fields)
    halo = exchange(sends)
    gram, merged = gram_call(basis, snapshots)
    halo, gram, merged = lax.optimization_barrier((halo, gram, merged))
    first = stage_call(0, odd, along_z, halo, fields, None)
    halo = exchange(first[3:])
    second = stage_call(1, odd, along_z, halo, first[:3], fields)
    halo = exchange(second[3:])
    final = stage_call(2, odd, along_z, halo, second[:3], fields)
    newest = final[3]
    parts = cross_call(merged, newest, gram, devices)
    parts = lax.all_to_all(parts, ("gx", "gy"), 0, 0, tiled=True)
    modes, factor = modes_call(parts, scale, merged, newest, weight)
    return (final[0], final[1], final[2], modes, factor)


def solution(mesh):
    field, vector = P("gx", "gy"), P(None, "gx", "gy")
    columns = P(None, None, "gx", "gy")
    return jax.shard_map(
        local,
        mesh=mesh,
        in_specs=(field, vector, field, columns, P(), columns),
        out_specs=(field, vector, field, columns, P()),
        check_vma=False,
    )
```

```python
import functools

import jax
import jax.numpy as jnp
import ml_dtypes
import numpy as np
from jax import lax
from jax.experimental import pallas as pl
from jax.experimental.pallas import tpu as pltpu
from jax.sharding import PartitionSpec as P

NZ = 64
LANES = 128
STEP_TIME = 0.03
FIRST = (0.8, -0.2, 4.0 / 105.0, -1.0 / 280.0)
SECOND = (8.0 / 5.0, -0.2, 8.0 / 315.0, -1.0 / 560.0)
CENTRAL = -205.0 / 72.0
UNROLL = (16, 16, 35, 16, 2, 4)
VMEM_LIMIT = 20 * 1024 * 1024
WHOLE = pl.BlockSpec(memory_space=pltpu.VMEM)
SCALAR = pl.BlockSpec(memory_space=pltpu.SMEM)


def lanes_at(index):
    return pl.ds(pl.multiple_of(index * LANES, LANES), LANES)


def loop(count, body, unroll=1):
    def group(i, carry):
        for n in range(unroll):
            body(i * unroll + n)
        return carry

    lax.fori_loop(0, count // unroll, group, 0)
    for n in range(count - count % unroll, count):
        body(n)


def row_ids():
    return lax.broadcasted_iota(jnp.int32, (8, LANES), 0)


def lane_ids():
    return lax.broadcasted_iota(jnp.int32, (8, LANES), 1)


def primitives(rho, mx, my, mz, energy):
    inv = 1.0 / rho
    u, v, w = mx * inv, my * inv, mz * inv
    p = 0.4 * (energy - 0.5 * (mx * u + my * v + mz * w))
    return u, v, w, p, p * inv


def low_rows(odd):
    return (row_ids() ^ (4 * odd[0])) < 4


def pack_sends(state, odd, to_far, to_near, first_y, last_y):
    length = state[0].shape[-1]
    half = length // (2 * LANES)
    low = low_rows(odd)

    def body(j):
        for f in range(5):
            here = state[f][:, lanes_at(j)]
            other = pltpu.roll(state[f][:, lanes_at(j + half)], 4, 0)
            to_far[f, :, lanes_at(j)] = jnp.where(low, here, other)
            to_near[f, :, lanes_at(j)] = jnp.where(low, other, here)

    loop(half, body, UNROLL[0])
    width = 4 * NZ
    for f in range(5):
        first_y[f] = state[f][:, :width]
        last_y[f] = state[f][:, length - width :]


def state_views(rho, mom, energy):
    return [rho, mom.at[0], mom.at[1], mom.at[2], energy]


def pack_kernel(odd, rho_h, mom_h, energy_h, z_h, rho, mom, energy, along_z, *rest):
    *sends, sems = rest
    pairs = ((rho_h, rho), (mom_h, mom), (energy_h, energy), (z_h, along_z))
    copies = [pltpu.make_async_copy(a, b, sems.at[i]) for i, (a, b) in enumerate(pairs)]
    for copy in copies:
        copy.start()
    for copy in copies:
        copy.wait()
    pack_sends(state_views(rho, mom, energy), odd, *sends)


def depth_weights():
    position = np.arange(LANES)
    same = position[:, None] // NZ == position[None, :] // NZ
    result = []
    for sign, coefficients in ((-1.0, FIRST), (1.0, SECOND)):
        full = np.zeros((LANES, LANES), np.float32)
        for k in range(1, 5):
            ahead = (position[None, :] + k - position[:, None]) % NZ == 0
            behind = (position[None, :] - k - position[:, None]) % NZ == 0
            full += coefficients[k - 1] * (same & ahead)
            full += sign * coefficients[k - 1] * (same & behind)
        hi = full.astype(ml_dtypes.bfloat16)
        lo = (full - hi.astype(np.float32)).astype(ml_dtypes.bfloat16)
        result.append(np.block([[hi, lo], [hi, np.zeros_like(lo)]]))
    return jnp.asarray(np.stack(result))


def values_along(fields, direction):
    r, mx, my, mz, e = fields
    u, v, w, p, t = primitives(r, mx, my, mz, e)
    along = (u, v, w)[direction]
    moved = [mx * along, my * along, mz * along]
    moved[direction] = moved[direction] + p
    mass = (mx, my, mz)[direction]
    return (mass, *moved, (e + p) * along, u, v, w, t, p)


def weighted(f, k, ahead, behind):
    if f < 5:
        return FIRST[k - 1] * (ahead - behind)
    return SECOND[k - 1] * (ahead + behind)


def half_step(here, following):
    return pltpu.roll(jnp.where(lane_ids() < NZ, following, here), NZ, 1)


def inner_kernel(along_z, rho, mom, energy, partial, ys, yh, zs, zd):
    state = state_views(rho, mom, energy)
    length = rho.shape[-1]
    blocks = length // LANES
    edge = 2 * LANES

    def fill(j):
        both = pl.ds(pl.multiple_of(j * edge, edge), edge)
        at = pl.ds(pl.multiple_of(j * edge + edge, edge), edge)
        place = pl.ds(pl.multiple_of(j * 16, 16), 16)
        fields = [s[:, both] for s in state]
        values = values_along(fields, 1)
        for f in range(10):
            ys[f, :, at] = values[f]
        u, v, w, t, p = values[5:]
        mx, my, mz, e = fields[1:]
        across = (mz, mx * w, my * w, mz * w + p, (e + p) * w, u, v, w, t)
        for f, value in enumerate(across):
            tall = jnp.concatenate([value[:, :LANES], value[:, LANES:]], 0)
            hi = tall.astype(jnp.bfloat16)
            zs[f, place, :LANES] = hi
            zs[f, place, LANES:] = (tall - hi.astype(jnp.float32)).astype(jnp.bfloat16)

    loop(blocks // 2, fill, UNROLL[1])
    for f in range(9):
        wide = jnp.dot(
            zs[f], along_z[0 if f < 5 else 1], preferred_element_type=jnp.float32
        )
        zd[f] = wide[:, :LANES] + wide[:, LANES:]
    empty = jnp.zeros((10, 8, edge), jnp.float32)
    ys[:, :, :edge] = empty
    ys[:, :, length + edge :] = empty

    def shift_half(j):
        for f in range(9):
            yh[f, :, lanes_at(j)] = half_step(ys[f, :, lanes_at(j)], ys[f, :, lanes_at(j + 1)])

    loop(blocks + 3, shift_half, UNROLL[2])

    def add(j):
        for f in range(9):
            total = zd[f, pl.ds(pl.multiple_of(j * 8, 8), 8), :]
            if f >= 5:
                total = total + (3.0 * CENTRAL) * ys[f, :, lanes_at(j + 2)]
            for k in range(1, 5):
                source = yh if k % 2 else ys
                ahead = source[f, :, lanes_at(j + 2 + k // 2)]
                behind = source[f, :, lanes_at(j + 2 - (k + 1) // 2)]
                total = total + weighted(f, k, ahead, behind)
            partial[f, :, lanes_at(j)] = total

    loop(blocks, add, UNROLL[5])


def outer_kernel(stage, refs):
    odd, partial_in, ys, far, near, before, after, rho, mom, energy = refs[:10]
    base = state_views(*refs[10:13]) if stage else None
    rest = refs[13:] if stage else refs[10:]
    rho_o, mom_o, energy_o, partial = rest[:4]
    if stage < 2:
        sends, hx = rest[4:8], rest[8]
    else:
        newest, hx = rest[4:]
    state = state_views(rho, mom, energy)
    outs = state_views(rho_o, mom_o, energy_o)
    length = rho.shape[-1]
    blocks = length // LANES
    half = blocks // 2
    row = row_ids()
    low = low_rows(odd)

    edges = []
    for halo in (before, after):
        edges.append(
            [
                values_along([halo[f, :, i * LANES : (i + 1) * LANES] for f in range(5)], 1)
                for i in range(2)
            ]
        )
    none = jnp.zeros((8, LANES), jnp.float32)
    for f in range(9):
        b0, b1 = edges[0][0][f], edges[0][1][f]
        a0, a1 = edges[1][0][f], edges[1][1][f]
        into, out_of = half_step(b1, none), half_step(none, a0)
        shares = {
            0: weighted(f, 1, none, into)
            + weighted(f, 2, none, b1)
            + weighted(f, 3, none, half_step(b0, b1))
            + weighted(f, 4, none, b0),
            1: weighted(f, 3, none, into) + weighted(f, 4, none, b1),
            blocks - 2: weighted(f, 3, out_of, none) + weighted(f, 4, a0, none),
            blocks - 1: weighted(f, 1, out_of, none)
            + weighted(f, 2, a0, none)
            + weighted(f, 3, half_step(a0, a1), none)
            + weighted(f, 4, a1, none),
        }
        for j, share in shares.items():
            at = slice(j * LANES, (j + 1) * LANES)
            partial[f, :, at] = partial_in[f, :, at] + share

    def unpack(j):
        for f in range(5):
            a, b = near[f, :, lanes_at(j)], far[f, :, lanes_at(j)]
            hx[f, :, lanes_at(j)] = jnp.where(low, a, b)
            hx[f, :, lanes_at(j + half)] = pltpu.roll(jnp.where(low, b, a), 4, 0)

    loop(half, unpack, UNROLL[3])

    def main(j):
        at = lanes_at(j)
        own = [s[:, at] for s in state]
        r, mx, my, mz, e = own
        u, v, w, t, p = [ys[5 + f, :, lanes_at(j + 2)] for f in range(5)]
        fx = (mx, mx * u + p, my * u, mz * u, (e + p) * u, u, v, w, t)
        hfx = values_along([hx[f, :, at] for f in range(5)], 0)
        result = []
        for f in range(9):
            total = partial[f, :, at]
            for k in range(1, 5):
                ahead = pltpu.roll(jnp.where(row < k, hfx[f], fx[f]), 8 - k, 0)
                behind = pltpu.roll(jnp.where(row >= 8 - k, hfx[f], fx[f]), k, 0)
                total = total + weighted(f, k, ahead, behind)
            result.append(total)
        visc = 0.08 * t
        lap = result[5:]
        work = visc * (u * lap[0] + v * lap[1] + w * lap[2] + 4.9 * lap[3])
        rate = [
            -result[0],
            visc * lap[0] - result[1],
            visc * lap[1] - result[2],
            visc * lap[2] - result[3],
            work - result[4],
        ]
        final = []
        for f in range(5):
            step = own[f] + STEP_TIME * rate[f]
            if stage == 1:
                step = 0.75 * base[f][:, at] + 0.25 * step
            elif stage == 2:
                step = base[f][:, at] * (1.0 / 3.0) + (2.0 / 3.0) * step
            outs[f][:, at] = step
            final.append(step)
        if stage == 2:
            inv = 1.0 / final[0]
            for c in range(3):
                newest[c, :, at] = final[1 + c] * inv

    loop(blocks, main, UNROLL[4])
    if stage < 2:
        pack_sends(outs, odd, *sends)


def f32(*shape):
    return jax.ShapeDtypeStruct(shape, jnp.float32)


def call(kernel, out_shape, args, scratch=(), flops=0, nbytes=0, vmem=VMEM_LIMIT, **kw):
    return pl.pallas_call(
        kernel,
        out_shape=out_shape,
        scratch_shapes=list(scratch),
        compiler_params=pltpu.CompilerParams(vmem_limit_bytes=vmem),
        cost_estimate=pl.CostEstimate(
            flops=flops, bytes_accessed=nbytes, transcendentals=0
        ),
        **kw,
    )(*args)


def in_hbm(*arrays):
    return tuple(pltpu.with_memory_space_constraint(a, pltpu.HBM) for a in arrays)


def state_shapes(rows, length):
    return (f32(rows, length), f32(3, rows, length), f32(rows, length))


def send_shapes(rows, length):
    packed = f32(5, rows, length // 2)
    edge = f32(5, rows, 4 * NZ)
    return (packed, packed, edge, edge)


def pack(odd, state):
    rows, length = state[0].shape
    weights = depth_weights()
    shapes = state_shapes(rows, length)
    shapes += (jax.ShapeDtypeStruct(weights.shape, weights.dtype),)
    shapes += send_shapes(rows, length)
    out = call(
        pack_kernel,
        shapes,
        (odd, *in_hbm(*state, weights)),
        [pltpu.SemaphoreType.DMA((4,))],
        in_specs=[SCALAR] + [pl.BlockSpec(memory_space=pltpu.HBM)] * 4,
        out_specs=[WHOLE] * 8,
        nbytes=10**6,
    )
    return out[:3], out[3], out[4:]


def inner_call(along_z, state):
    rows, length = state[0].shape
    padded = length + 8 * NZ
    return call(
        inner_kernel,
        (f32(9, rows, length), f32(10, rows, padded)),
        (along_z, *state),
        [
            pltpu.VMEM((9, rows, padded), jnp.float32),
            pltpu.VMEM((9, length // 16, 2 * LANES), jnp.bfloat16),
            pltpu.VMEM((9, length // 16, LANES), jnp.float32),
        ],
        in_specs=[WHOLE] * 4,
        out_specs=[WHOLE] * 2,
        flops=32768 * 400,
        nbytes=3 * 10**6,
    )


def outer_call(stage, odd, inner, halo, state, base):
    rows, length = state[0].shape
    out = state_shapes(rows, length) + (f32(9, rows, length),)
    out += send_shapes(rows, length) if stage < 2 else (f32(3, rows, length),)
    args = (odd, *inner, *halo, *state) + (tuple(base) if stage else ())
    out = call(
        lambda *refs: outer_kernel(stage, refs),
        out,
        args,
        [pltpu.VMEM((5, rows, length), jnp.float32)],
        in_specs=[SCALAR] + [WHOLE] * (len(args) - 1),
        out_specs=[WHOLE] * len(out),
        input_output_aliases={1: 3},
        flops=32768 * 400,
        nbytes=3 * 10**6,
    )
    return out[:3], out[4:]


def merged_rows(basis, snaps, c, at):
    first = basis[:, c, :, at].astype(jnp.float32)
    second = snaps[:, c, :, at].astype(jnp.float32)
    length = first.shape[-1]
    rows = jnp.concatenate([first, second, jnp.zeros((1, 8, length), jnp.float32)], 0)
    return rows.reshape(256, length).astype(jnp.bfloat16)


def group_matrix(shape, group_dim, dtype):
    g = lax.broadcasted_iota(jnp.int32, shape, group_dim)
    o = lax.broadcasted_iota(jnp.int32, shape, 1 - group_dim)
    return (g // 8 == o).astype(dtype)


def same_layer():
    r = lax.broadcasted_iota(jnp.int32, (256, 256), 0)
    c = lax.broadcasted_iota(jnp.int32, (256, 256), 1)
    return r % 8 == c % 8


def pack_square(small):
    return jnp.concatenate([small[8 * g : 8 * g + 8] for g in range(4)], 1)


GRAM_WIDTH = 1024


def gram_kernel(part, basis_h, snaps_h, gram, merged, basis, snaps, total, sems):
    width = GRAM_WIDTH
    start = part * merged.shape[-1]
    places = [slice(i, i + width) for i in range(0, merged.shape[-1], width)]
    loads = []
    for n, at in enumerate(places):
        for m, (source, held) in enumerate(((basis_h, basis), (snaps_h, snaps))):
            loads.append(
                pltpu.make_async_copy(
                    source.at[:, :, :, start + at.start : start + at.stop],
                    held.at[:, :, :, at],
                    sems.at[n, m],
                )
            )
            loads[-1].start()
    total[...] = jnp.zeros_like(total)
    for n, at in enumerate(places):
        loads[2 * n].wait()
        loads[2 * n + 1].wait()
        for c in range(3):
            rows = merged_rows(basis, snaps, c, at)
            merged[c, :, at] = rows
            total[...] += lax.dot_general(
                rows, rows, (((1,), (1,)), ((), ())), preferred_element_type=jnp.float32
            )
    kept = jnp.where(same_layer(), total[...], 0.0)
    left = group_matrix((32, 256), 1, jnp.float32)
    right = group_matrix((256, 32), 0, jnp.float32)
    small = jnp.dot(left, kept, precision=lax.Precision.HIGHEST)
    small = jnp.dot(small, right, precision=lax.Precision.HIGHEST)
    gram[...] = pack_square(small)


def gram_call(basis, snaps, part):
    length = basis.shape[-1] // 2
    hbm = pl.BlockSpec(memory_space=pltpu.HBM)
    return call(
        functools.partial(gram_kernel, part),
        (f32(8, LANES), pltpu.VMEM((3, 256, length), jnp.bfloat16)),
        in_hbm(basis, snaps),
        [
            pltpu.VMEM((*basis.shape[:-1], length), jnp.bfloat16),
            pltpu.VMEM((*snaps.shape[:-1], length), jnp.bfloat16),
            pltpu.VMEM((256, 256), jnp.float32),
            pltpu.SemaphoreType.DMA((length // GRAM_WIDTH, 2)),
        ],
        in_specs=[hbm, hbm],
        out_specs=[WHOLE] * 2,
        flops=2 * 256 * 256 * 3 * length,
        nbytes=31 * 3 * 8 * length * 2,
    )


def cross_kernel(merged_a, merged_b, newest, gram_a, gram_b, parts, total):
    blocks = newest.shape[-1] // LANES
    half = blocks // 2

    def add(i):
        pair = pl.ds(pl.multiple_of(i * 16, 16), 16)
        sums = [jnp.zeros((2, 8, LANES), jnp.float32) for _ in range(4)]
        for n in range(3 * blocks):
            c, at = n % 3, slice(n // 3 * LANES, (n // 3 + 1) * LANES)
            merged = merged_a if n // 3 < half else merged_b
            first = n // 3 % half * LANES
            rows = merged[c, pair, first : first + LANES]
            rows = rows.astype(jnp.float32).reshape(2, 8, LANES)
            sums[n % 4] = sums[n % 4] + rows * newest[c, :, at]
        total[pl.ds(i * 2, 2)] = (sums[0] + sums[1]) + (sums[2] + sums[3])

    loop(16, add)
    own = [jnp.zeros((8, LANES), jnp.float32) for _ in range(4)]
    for n in range(3 * blocks):
        value = newest[n % 3, :, n // 3 * LANES : (n // 3 + 1) * LANES]
        own[n % 4] = own[n % 4] + value * value
    total[31] = (own[0] + own[1]) + (own[2] + own[3])
    sums = jnp.sum(total[...], axis=1)
    line = lax.dot_general(
        jnp.ones((8, LANES), jnp.float32),
        sums,
        (((1,), (1,)), ((), ())),
        precision=lax.Precision.HIGHEST,
    )
    line = jnp.concatenate([jnp.zeros((8, 96), jnp.float32), line], 1)
    last = (row_ids() == 7) & (lane_ids() >= 96)
    parts[...] = jnp.where(last, line, gram_a[...] + gram_b[...])


def cross_call(merged, newest, grams):
    length = newest.shape[-1]
    return call(
        cross_kernel,
        f32(8, LANES),
        (*merged, newest, *grams),
        [pltpu.VMEM((32, 8, LANES), jnp.float32)],
        in_specs=[WHOLE] * 5,
        out_specs=WHOLE,
        flops=31 * 6 * 8 * length,
        nbytes=31 * 3 * 8 * length * 2,
    )


def eliminated(work):
    wide = (8, LANES)
    blocks = [work[8 * i : 8 * i + 8] for i in range(4)]
    row = row_ids()
    done = []
    for b in range(4):
        columns = [
            {i: jnp.broadcast_to(blocks[i][:, 8 * b + s : 8 * b + s + 1], wide) for i in range(b, 4)}
            for s in range(8)
        ]
        rows = [jnp.broadcast_to(blocks[b][s : s + 1], wide) for s in range(8)]
        result = jnp.zeros(wide, jnp.float32)
        scaled = []
        for t in range(8):
            pivot = jnp.broadcast_to(columns[t][b][t : t + 1], wide)
            inv = 1.0 / pivot
            result = jnp.where(row == t, rows[t] / jnp.sqrt(pivot), result)
            scaled.append(rows[t] * inv)
            for s in range(t + 1, 8):
                ratio = jnp.broadcast_to(columns[s][b][t : t + 1], wide) * inv
                below = jnp.broadcast_to(columns[t][b][s : s + 1], wide)
                rows[s] = rows[s] - below * scaled[t]
                for i in range(b, 4):
                    columns[s][i] = columns[s][i] - columns[t][i] * ratio
        done.append(result)
        for i in range(b + 1, 4):
            for t in range(8):
                blocks[i] = blocks[i] - columns[t][i] * scaled[t]
    return jnp.concatenate(done, 0)


def weights_of(weight, parts, scale, factor, high, low, diagonal):
    row = lax.broadcasted_iota(jnp.int32, (32, 32), 0)
    col = lax.broadcasted_iota(jnp.int32, (32, 32), 1)
    s = jnp.broadcast_to(scale[...], (32, 32))
    s_col = jnp.sum(jnp.where(row == col, s, 0.0), axis=1, keepdims=True)
    packed = jnp.sum(parts[...], axis=0)
    g = jnp.concatenate([packed[:, 32 * i : 32 * i + 32] for i in range(4)], 0)
    line = jnp.broadcast_to(g[31:32], (32, 32))
    line = jnp.sum(jnp.where(row == col, line, 0.0), axis=1, keepdims=True)
    g = jnp.where(col == 31, line, g)
    g = g * (weight * s) * s_col
    eye = (row == col).astype(jnp.float32)
    done = eliminated(jnp.concatenate([g, eye, jnp.zeros((32, 64), jnp.float32)], 1))
    factor[...] = jnp.where(col >= row, done[:, :32], 0.0)
    l = jnp.where(col <= row, done[:, 32:64], 0.0)
    diagonal[...] = jnp.broadcast_to(l[31:32, 31:32], diagonal.shape)
    scaled = jnp.where(col < 31, l * s, 0.0)
    hi = scaled.astype(jnp.bfloat16)
    lo = (scaled - hi.astype(jnp.float32)).astype(jnp.bfloat16)
    left = group_matrix((256, 32), 0, jnp.bfloat16)
    right = group_matrix((32, 256), 1, jnp.bfloat16)
    keep = same_layer()
    for part, out in ((hi, high), (lo, low)):
        wide = jnp.dot(left, part, preferred_element_type=jnp.float32)
        wide = jnp.dot(
            wide.astype(jnp.bfloat16), right, preferred_element_type=jnp.float32
        )
        out[...] = jnp.where(keep, wide, 0.0).astype(jnp.bfloat16)


def modes_kernel(
    weight,
    parts,
    scale,
    merged_a,
    merged_b,
    newest,
    modes,
    factor,
    merged,
    out,
    high,
    low,
    diagonal,
    in_sems,
    out_sems,
):
    width = newest.shape[-1] // 2
    pieces = [(3 * i + c, i, c) for i in range(2) for c in range(3)]
    loads = [
        pltpu.make_async_copy((merged_a, merged_b)[i].at[c], merged.at[n], in_sems.at[n])
        for n, i, c in pieces
    ]
    for load in loads[:3]:
        load.start()
    weights_of(weight, parts, scale, factor, high, low, diagonal)
    for load in loads[3:]:
        load.start()
    stores = []
    for n, i, c in pieces:
        loads[n].wait()
        at = slice(i * width, (i + 1) * width)
        rows = merged[n]
        value = jnp.dot(high[...], rows, preferred_element_type=jnp.float32)
        value = value + jnp.dot(low[...], rows, preferred_element_type=jnp.float32)
        value = value.reshape(32, 8, width)
        out[:31, c, :, at] = value[:31].astype(jnp.bfloat16)
        own = diagonal[:, :1] * newest[c, :, at]
        out[31, c, :, at] = (value[31] + own).astype(jnp.bfloat16)
        store = pltpu.make_async_copy(
            out.at[:, c, :, at], modes.at[:, c, :, at], out_sems.at[n]
        )
        store.start()
        stores.append(store)
    for store in stores:
        store.wait()


def modes_call(parts, scale, merged, newest, weight):
    length = newest.shape[-1]
    shape = (32, 3, 8, length)
    hbm = pl.BlockSpec(memory_space=pltpu.HBM)
    return call(
        functools.partial(modes_kernel, weight),
        (jax.ShapeDtypeStruct(shape, jnp.bfloat16), f32(32, 32)),
        (parts, scale, *in_hbm(*merged), newest),
        [
            pltpu.VMEM((6, 256, length // 2), jnp.bfloat16),
            pltpu.VMEM(shape, jnp.bfloat16),
            pltpu.VMEM((256, 256), jnp.bfloat16),
            pltpu.VMEM((256, 256), jnp.bfloat16),
            pltpu.VMEM((8, LANES), jnp.float32),
            pltpu.SemaphoreType.DMA((6,)),
            pltpu.SemaphoreType.DMA((6,)),
        ],
        in_specs=[WHOLE, WHOLE, hbm, hbm, WHOLE],
        out_specs=[hbm, WHOLE],
        flops=4 * 256 * 256 * 3 * length,
        nbytes=63 * 3 * 8 * length * 2,
    )


def shifted(block, axis, distance):
    count = lax.axis_size(axis)
    route = [(i, (i + distance) % count) for i in range(count)]
    return lax.ppermute(block, axis, route)


def exchange(sends):
    to_far, to_near, first_y, last_y = sends
    count = lax.axis_size("gx")
    pairs = [(i, (i + 1) % count) for i in range(1, count, 2)]
    far = lax.ppermute(to_far, "gx", pairs + [(j, i) for i, j in pairs])
    near = lax.ppermute(to_near, "gx", [(i, i ^ 1) for i in range(count)])
    before = shifted(last_y, "gy", 1)
    after = shifted(first_y, "gy", -1)
    return (far, near, before, after)


def total_parts(part):
    count, other = lax.axis_size("gx"), lax.axis_size("gy")
    part = part + lax.ppermute(part, "gx", [(i, i ^ 1) for i in range(count)])
    groups = [
        [i for i in range(count * other) if i // other % 2 == core] for core in range(2)
    ]
    copies = jnp.broadcast_to(part[None], (count * other // 2, *part.shape))
    return lax.all_to_all(
        copies, ("gx", "gy"), 0, 0, tiled=True, axis_index_groups=groups
    )


def local(density, momentum, energy, basis, scales, snapshots):
    rows, length = density.shape
    devices = lax.axis_size("gx") * lax.axis_size("gy")
    weight = 1.0 / (3 * rows * length * devices)
    fields = (density, momentum, energy)
    scale = jnp.concatenate([scales, jnp.ones((16,), jnp.float32)])[None]

    odd = (lax.axis_index("gx") % 2).astype(jnp.int32)[None]
    fields, along_z, sends = pack(odd, fields)
    halo, inner = exchange(sends), inner_call(along_z, fields)
    state, sends = outer_call(0, odd, inner, halo, fields, None)
    old = []
    for stage in (1, 2):
        halo, inner = exchange(sends), inner_call(along_z, state)
        old.append(gram_call(basis, snapshots, stage - 1))
        halo, inner, old = lax.optimization_barrier((halo, inner, old))
        state, sends = outer_call(stage, odd, inner, halo, state, fields)
    final, (newest,) = state, sends
    grams, merged = zip(*old)
    parts = total_parts(cross_call(merged, newest, grams))
    modes, factor = modes_call(parts, scale, merged, newest, weight)
    return (final[0], final[1], final[2], modes, factor)


def solution(mesh):
    field, vector = P("gx", "gy"), P(None, "gx", "gy")
    columns = P(None, None, "gx", "gy")
    return jax.shard_map(
        local,
        mesh=mesh,
        in_specs=(field, vector, field, columns, P(), columns),
        out_specs=(field, vector, field, columns, P()),
        check_vma=False,
    )
```

```python
import functools

import jax
import jax.numpy as jnp
import ml_dtypes
import numpy as np
from jax import lax
from jax.experimental import pallas as pl
from jax.experimental.pallas import tpu as pltpu
from jax.sharding import PartitionSpec as P

NZ = 64
LANES = 128
STEP_TIME = 0.03
FIRST = (0.8, -0.2, 4.0 / 105.0, -1.0 / 280.0)
SECOND = (8.0 / 5.0, -0.2, 8.0 / 315.0, -1.0 / 560.0)
CENTRAL = -205.0 / 72.0
UNROLL = (16, 16, 35, 16, 8, 16)
VMEM_LIMIT = 20 * 1024 * 1024
WHOLE = pl.BlockSpec(memory_space=pltpu.VMEM)
SCALAR = pl.BlockSpec(memory_space=pltpu.SMEM)


def lanes_at(index):
    return pl.ds(pl.multiple_of(index * LANES, LANES), LANES)


def loop(count, body, unroll=1):
    def group(i, carry):
        for n in range(unroll):
            body(i * unroll + n)
        return carry

    lax.fori_loop(0, count // unroll, group, 0)
    for n in range(count - count % unroll, count):
        body(n)


def row_ids():
    return lax.broadcasted_iota(jnp.int32, (8, LANES), 0)


def lane_ids():
    return lax.broadcasted_iota(jnp.int32, (8, LANES), 1)


def primitives(rho, mx, my, mz, energy):
    inv = 1.0 / rho
    u, v, w = mx * inv, my * inv, mz * inv
    p = 0.4 * (energy - 0.5 * (mx * u + my * v + mz * w))
    return u, v, w, p, p * inv


def low_rows(odd):
    return (row_ids() ^ (4 * odd[0])) < 4


def pack_sends(state, odd, to_far, to_near, first_y, last_y):
    length = state[0].shape[-1]
    half = length // (2 * LANES)
    low = low_rows(odd)

    def body(j):
        for f in range(5):
            here = state[f][:, lanes_at(j)]
            other = pltpu.roll(state[f][:, lanes_at(j + half)], 4, 0)
            to_far[f, :, lanes_at(j)] = jnp.where(low, here, other)
            to_near[f, :, lanes_at(j)] = jnp.where(low, other, here)

    loop(half, body, UNROLL[0])
    width = 4 * NZ
    for f in range(5):
        first_y[f] = state[f][:, :width]
        last_y[f] = state[f][:, length - width :]


def state_views(rho, mom, energy):
    return [rho, mom.at[0], mom.at[1], mom.at[2], energy]


def pack_kernel(odd, rho_h, mom_h, energy_h, z_h, rho, mom, energy, along_z, *rest):
    *sends, sems = rest
    pairs = ((rho_h, rho), (mom_h, mom), (energy_h, energy), (z_h, along_z))
    copies = [pltpu.make_async_copy(a, b, sems.at[i]) for i, (a, b) in enumerate(pairs)]
    for copy in copies:
        copy.start()
    for copy in copies:
        copy.wait()
    pack_sends(state_views(rho, mom, energy), odd, *sends)


def depth_weights():
    position = np.arange(LANES)
    same = position[:, None] // NZ == position[None, :] // NZ
    result = []
    for sign, coefficients in ((-1.0, FIRST), (1.0, SECOND)):
        full = np.zeros((LANES, LANES), np.float32)
        for k in range(1, 5):
            ahead = (position[None, :] + k - position[:, None]) % NZ == 0
            behind = (position[None, :] - k - position[:, None]) % NZ == 0
            full += coefficients[k - 1] * (same & ahead)
            full += sign * coefficients[k - 1] * (same & behind)
        hi = full.astype(ml_dtypes.bfloat16)
        lo = (full - hi.astype(np.float32)).astype(ml_dtypes.bfloat16)
        result.append(np.block([[hi, lo], [hi, np.zeros_like(lo)]]))
    return jnp.asarray(np.stack(result))


def values_along(fields, direction):
    r, mx, my, mz, e = fields
    u, v, w, p, t = primitives(r, mx, my, mz, e)
    along = (u, v, w)[direction]
    moved = [mx * along, my * along, mz * along]
    moved[direction] = moved[direction] + p
    mass = (mx, my, mz)[direction]
    return (mass, *moved, (e + p) * along, u, v, w, t, p)


def weighted(f, k, ahead, behind):
    if f < 5:
        return FIRST[k - 1] * (ahead - behind)
    return SECOND[k - 1] * (ahead + behind)


def half_step(here, following):
    return pltpu.roll(jnp.where(lane_ids() < NZ, following, here), NZ, 1)


def inner_kernel(along_z, rho, mom, energy, partial, ys, yh, zs, zd):
    state = state_views(rho, mom, energy)
    length = rho.shape[-1]
    blocks = length // LANES
    edge = 2 * LANES

    def fill(j):
        both = pl.ds(pl.multiple_of(j * edge, edge), edge)
        at = pl.ds(pl.multiple_of(j * edge + edge, edge), edge)
        place = pl.ds(pl.multiple_of(j * 16, 16), 16)
        fields = [s[:, both] for s in state]
        values = values_along(fields, 1)
        for f in range(10):
            ys[f, :, at] = values[f]
        u, v, w, t, p = values[5:]
        mx, my, mz, e = fields[1:]
        across = (mz, mx * w, my * w, mz * w + p, (e + p) * w, u, v, w, t)
        for f, value in enumerate(across):
            tall = jnp.concatenate([value[:, :LANES], value[:, LANES:]], 0)
            hi = tall.astype(jnp.bfloat16)
            zs[f, place, :LANES] = hi
            zs[f, place, LANES:] = (tall - hi.astype(jnp.float32)).astype(jnp.bfloat16)

    loop(blocks // 2, fill, UNROLL[1])
    for f in range(9):
        wide = jnp.dot(
            zs[f], along_z[0 if f < 5 else 1], preferred_element_type=jnp.float32
        )
        zd[f] = wide[:, :LANES] + wide[:, LANES:]
    empty = jnp.zeros((10, 8, edge), jnp.float32)
    ys[:, :, :edge] = empty
    ys[:, :, length + edge :] = empty

    def shift_half(j):
        for f in range(9):
            yh[f, :, lanes_at(j)] = half_step(ys[f, :, lanes_at(j)], ys[f, :, lanes_at(j + 1)])

    loop(blocks + 3, shift_half, UNROLL[2])

    def add(j):
        for f in range(9):
            total = zd[f, pl.ds(pl.multiple_of(j * 8, 8), 8), :]
            if f >= 5:
                total = total + (3.0 * CENTRAL) * ys[f, :, lanes_at(j + 2)]
            for k in range(1, 5):
                source = yh if k % 2 else ys
                ahead = source[f, :, lanes_at(j + 2 + k // 2)]
                behind = source[f, :, lanes_at(j + 2 - (k + 1) // 2)]
                total = total + weighted(f, k, ahead, behind)
            partial[f, :, lanes_at(j)] = total

    loop(blocks, add, UNROLL[5])


def outer_kernel(stage, refs):
    odd, partial_in, ys, far, near, before, after, rho, mom, energy = refs[:10]
    base = state_views(*refs[10:13]) if stage else None
    rest = refs[13:] if stage else refs[10:]
    rho_o, mom_o, energy_o, partial = rest[:4]
    if stage < 2:
        sends, hx = rest[4:8], rest[8]
    else:
        newest, hx = rest[4:]
    state = state_views(rho, mom, energy)
    outs = state_views(rho_o, mom_o, energy_o)
    length = rho.shape[-1]
    blocks = length // LANES
    half = blocks // 2
    row = row_ids()
    low = low_rows(odd)

    edges = []
    for halo in (before, after):
        edges.append(
            [
                values_along([halo[f, :, i * LANES : (i + 1) * LANES] for f in range(5)], 1)
                for i in range(2)
            ]
        )
    none = jnp.zeros((8, LANES), jnp.float32)
    for f in range(9):
        b0, b1 = edges[0][0][f], edges[0][1][f]
        a0, a1 = edges[1][0][f], edges[1][1][f]
        into, out_of = half_step(b1, none), half_step(none, a0)
        shares = {
            0: weighted(f, 1, none, into)
            + weighted(f, 2, none, b1)
            + weighted(f, 3, none, half_step(b0, b1))
            + weighted(f, 4, none, b0),
            1: weighted(f, 3, none, into) + weighted(f, 4, none, b1),
            blocks - 2: weighted(f, 3, out_of, none) + weighted(f, 4, a0, none),
            blocks - 1: weighted(f, 1, out_of, none)
            + weighted(f, 2, a0, none)
            + weighted(f, 3, half_step(a0, a1), none)
            + weighted(f, 4, a1, none),
        }
        for j, share in shares.items():
            at = slice(j * LANES, (j + 1) * LANES)
            partial[f, :, at] = partial_in[f, :, at] + share

    def unpack(j):
        for f in range(5):
            a, b = near[f, :, lanes_at(j)], far[f, :, lanes_at(j)]
            hx[f, :, lanes_at(j)] = jnp.where(low, a, b)
            hx[f, :, lanes_at(j + half)] = pltpu.roll(jnp.where(low, b, a), 4, 0)

    loop(half, unpack, UNROLL[3])

    def main(j):
        at = lanes_at(j)
        own = [s[:, at] for s in state]
        r, mx, my, mz, e = own
        u, v, w, t, p = [ys[5 + f, :, lanes_at(j + 2)] for f in range(5)]
        fx = (mx, mx * u + p, my * u, mz * u, (e + p) * u, u, v, w, t)
        hfx = values_along([hx[f, :, at] for f in range(5)], 0)
        result = []
        for f in range(9):
            total = partial[f, :, at]
            for k in range(1, 5):
                ahead = pltpu.roll(jnp.where(row < k, hfx[f], fx[f]), 8 - k, 0)
                behind = pltpu.roll(jnp.where(row >= 8 - k, hfx[f], fx[f]), k, 0)
                total = total + weighted(f, k, ahead, behind)
            result.append(total)
        visc = 0.08 * t
        lap = result[5:]
        work = visc * (u * lap[0] + v * lap[1] + w * lap[2] + 4.9 * lap[3])
        rate = [
            -result[0],
            visc * lap[0] - result[1],
            visc * lap[1] - result[2],
            visc * lap[2] - result[3],
            work - result[4],
        ]
        final = []
        for f in range(5):
            step = own[f] + STEP_TIME * rate[f]
            if stage == 1:
                step = 0.75 * base[f][:, at] + 0.25 * step
            elif stage == 2:
                step = base[f][:, at] * (1.0 / 3.0) + (2.0 / 3.0) * step
            outs[f][:, at] = step
            final.append(step)
        if stage == 2:
            inv = 1.0 / final[0]
            for c in range(3):
                newest[c, :, at] = final[1 + c] * inv

    loop(blocks, main, UNROLL[4])
    if stage < 2:
        pack_sends(outs, odd, *sends)


def f32(*shape):
    return jax.ShapeDtypeStruct(shape, jnp.float32)


def call(kernel, out_shape, args, scratch=(), flops=0, nbytes=0, vmem=VMEM_LIMIT, **kw):
    return pl.pallas_call(
        kernel,
        out_shape=out_shape,
        scratch_shapes=list(scratch),
        compiler_params=pltpu.CompilerParams(vmem_limit_bytes=vmem),
        cost_estimate=pl.CostEstimate(
            flops=flops, bytes_accessed=nbytes, transcendentals=0
        ),
        **kw,
    )(*args)


def in_hbm(*arrays):
    return tuple(pltpu.with_memory_space_constraint(a, pltpu.HBM) for a in arrays)


def state_shapes(rows, length):
    return (f32(rows, length), f32(3, rows, length), f32(rows, length))


def send_shapes(rows, length):
    packed = f32(5, rows, length // 2)
    edge = f32(5, rows, 4 * NZ)
    return (packed, packed, edge, edge)


def pack(odd, state):
    rows, length = state[0].shape
    weights = depth_weights()
    shapes = state_shapes(rows, length)
    shapes += (jax.ShapeDtypeStruct(weights.shape, weights.dtype),)
    shapes += send_shapes(rows, length)
    out = call(
        pack_kernel,
        shapes,
        (odd, *in_hbm(*state, weights)),
        [pltpu.SemaphoreType.DMA((4,))],
        in_specs=[SCALAR] + [pl.BlockSpec(memory_space=pltpu.HBM)] * 4,
        out_specs=[WHOLE] * 8,
        nbytes=10**6,
    )
    return out[:3], out[3], out[4:]


def inner_call(along_z, state):
    rows, length = state[0].shape
    padded = length + 8 * NZ
    return call(
        inner_kernel,
        (f32(9, rows, length), f32(10, rows, padded)),
        (along_z, *state),
        [
            pltpu.VMEM((9, rows, padded), jnp.float32),
            pltpu.VMEM((9, length // 16, 2 * LANES), jnp.bfloat16),
            pltpu.VMEM((9, length // 16, LANES), jnp.float32),
        ],
        in_specs=[WHOLE] * 4,
        out_specs=[WHOLE] * 2,
        flops=32768 * 400,
        nbytes=3 * 10**6,
    )


def outer_call(stage, odd, inner, halo, state, base):
    rows, length = state[0].shape
    out = state_shapes(rows, length) + (f32(9, rows, length),)
    out += send_shapes(rows, length) if stage < 2 else (f32(3, rows, length),)
    args = (odd, *inner, *halo, *state) + (tuple(base) if stage else ())
    out = call(
        lambda *refs: outer_kernel(stage, refs),
        out,
        args,
        [pltpu.VMEM((5, rows, length), jnp.float32)],
        in_specs=[SCALAR] + [WHOLE] * (len(args) - 1),
        out_specs=[WHOLE] * len(out),
        input_output_aliases={1: 3},
        flops=32768 * 400,
        nbytes=3 * 10**6,
    )
    return out[:3], out[4:]


def merged_rows(basis, snaps, c, at):
    first = basis[:, c, :, at].astype(jnp.float32)
    second = snaps[:, c, :, at].astype(jnp.float32)
    length = first.shape[-1]
    rows = jnp.concatenate([first, second, jnp.zeros((1, 8, length), jnp.float32)], 0)
    return rows.reshape(256, length).astype(jnp.bfloat16)


def group_matrix(shape, group_dim, dtype):
    g = lax.broadcasted_iota(jnp.int32, shape, group_dim)
    o = lax.broadcasted_iota(jnp.int32, shape, 1 - group_dim)
    return (g // 8 == o).astype(dtype)


def same_layer():
    r = lax.broadcasted_iota(jnp.int32, (256, 256), 0)
    c = lax.broadcasted_iota(jnp.int32, (256, 256), 1)
    return r % 8 == c % 8


def pack_square(small):
    return jnp.concatenate([small[8 * g : 8 * g + 8] for g in range(4)], 1)


GRAM_WIDTH = 1024


def gram_kernel(part, basis_h, snaps_h, gram, merged, basis, snaps, total, sems):
    width = GRAM_WIDTH
    start = part * merged.shape[-1]
    places = [slice(i, i + width) for i in range(0, merged.shape[-1], width)]
    loads = []
    for n, at in enumerate(places):
        for m, (source, held) in enumerate(((basis_h, basis), (snaps_h, snaps))):
            loads.append(
                pltpu.make_async_copy(
                    source.at[:, :, :, start + at.start : start + at.stop],
                    held.at[:, :, :, at],
                    sems.at[n, m],
                )
            )
            loads[-1].start()
    total[...] = jnp.zeros_like(total)
    for n, at in enumerate(places):
        loads[2 * n].wait()
        loads[2 * n + 1].wait()
        for c in range(3):
            rows = merged_rows(basis, snaps, c, at)
            merged[c, :, at] = rows
            total[...] += lax.dot_general(
                rows, rows, (((1,), (1,)), ((), ())), preferred_element_type=jnp.float32
            )
    kept = jnp.where(same_layer(), total[...], 0.0)
    left = group_matrix((32, 256), 1, jnp.float32)
    right = group_matrix((256, 32), 0, jnp.float32)
    small = jnp.dot(left, kept, precision=lax.Precision.HIGHEST)
    small = jnp.dot(small, right, precision=lax.Precision.HIGHEST)
    gram[...] = pack_square(small)


def gram_call(basis, snaps, part):
    length = basis.shape[-1] // 2
    hbm = pl.BlockSpec(memory_space=pltpu.HBM)
    return call(
        functools.partial(gram_kernel, part),
        (f32(8, LANES), pltpu.VMEM((3, 256, length), jnp.bfloat16)),
        in_hbm(basis, snaps),
        [
            pltpu.VMEM((*basis.shape[:-1], length), jnp.bfloat16),
            pltpu.VMEM((*snaps.shape[:-1], length), jnp.bfloat16),
            pltpu.VMEM((256, 256), jnp.float32),
            pltpu.SemaphoreType.DMA((length // GRAM_WIDTH, 2)),
        ],
        in_specs=[hbm, hbm],
        out_specs=[WHOLE] * 2,
        flops=2 * 256 * 256 * 3 * length,
        nbytes=31 * 3 * 8 * length * 2,
    )


def cross_kernel(merged_a, merged_b, newest, gram_a, gram_b, parts, total):
    blocks = newest.shape[-1] // LANES
    half = blocks // 2

    def add(i):
        pair = pl.ds(pl.multiple_of(i * 16, 16), 16)
        sums = [jnp.zeros((2, 8, LANES), jnp.float32) for _ in range(4)]
        for n in range(3 * blocks):
            c, at = n % 3, slice(n // 3 * LANES, (n // 3 + 1) * LANES)
            merged = merged_a if n // 3 < half else merged_b
            first = n // 3 % half * LANES
            rows = merged[c, pair, first : first + LANES]
            rows = rows.astype(jnp.float32).reshape(2, 8, LANES)
            sums[n % 4] = sums[n % 4] + rows * newest[c, :, at]
        total[pl.ds(i * 2, 2)] = (sums[0] + sums[1]) + (sums[2] + sums[3])

    loop(16, add)
    own = [jnp.zeros((8, LANES), jnp.float32) for _ in range(4)]
    for n in range(3 * blocks):
        value = newest[n % 3, :, n // 3 * LANES : (n // 3 + 1) * LANES]
        own[n % 4] = own[n % 4] + value * value
    total[31] = (own[0] + own[1]) + (own[2] + own[3])
    sums = jnp.sum(total[...], axis=1)
    line = lax.dot_general(
        jnp.ones((8, LANES), jnp.float32),
        sums,
        (((1,), (1,)), ((), ())),
        precision=lax.Precision.HIGHEST,
    )
    line = jnp.concatenate([jnp.zeros((8, 96), jnp.float32), line], 1)
    last = (row_ids() == 7) & (lane_ids() >= 96)
    parts[...] = jnp.where(last, line, gram_a[...] + gram_b[...])


def cross_call(merged, newest, grams):
    length = newest.shape[-1]
    return call(
        cross_kernel,
        f32(8, LANES),
        (*merged, newest, *grams),
        [pltpu.VMEM((32, 8, LANES), jnp.float32)],
        in_specs=[WHOLE] * 5,
        out_specs=WHOLE,
        flops=31 * 6 * 8 * length,
        nbytes=31 * 3 * 8 * length * 2,
    )


def eliminated(work):
    wide = (8, LANES)
    blocks = [work[8 * i : 8 * i + 8] for i in range(4)]
    row = row_ids()
    done = []
    for b in range(4):
        columns = [
            {i: jnp.broadcast_to(blocks[i][:, 8 * b + s : 8 * b + s + 1], wide) for i in range(b, 4)}
            for s in range(8)
        ]
        rows = [jnp.broadcast_to(blocks[b][s : s + 1], wide) for s in range(8)]
        result = jnp.zeros(wide, jnp.float32)
        scaled = []
        for t in range(8):
            pivot = jnp.broadcast_to(columns[t][b][t : t + 1], wide)
            inv = 1.0 / pivot
            result = jnp.where(row == t, rows[t] / jnp.sqrt(pivot), result)
            scaled.append(rows[t] * inv)
            for s in range(t + 1, 8):
                ratio = jnp.broadcast_to(columns[s][b][t : t + 1], wide) * inv
                below = jnp.broadcast_to(columns[t][b][s : s + 1], wide)
                rows[s] = rows[s] - below * scaled[t]
                for i in range(b, 4):
                    columns[s][i] = columns[s][i] - columns[t][i] * ratio
        done.append(result)
        for i in range(b + 1, 4):
            for t in range(8):
                blocks[i] = blocks[i] - columns[t][i] * scaled[t]
    return jnp.concatenate(done, 0)


def weights_of(weight, parts, scale, factor, high, low, diagonal):
    row = lax.broadcasted_iota(jnp.int32, (32, 32), 0)
    col = lax.broadcasted_iota(jnp.int32, (32, 32), 1)
    s = jnp.broadcast_to(scale[...], (32, 32))
    s_col = jnp.sum(jnp.where(row == col, s, 0.0), axis=1, keepdims=True)
    packed = jnp.sum(parts[...], axis=0)
    g = jnp.concatenate([packed[:, 32 * i : 32 * i + 32] for i in range(4)], 0)
    line = jnp.broadcast_to(g[31:32], (32, 32))
    line = jnp.sum(jnp.where(row == col, line, 0.0), axis=1, keepdims=True)
    g = jnp.where(col == 31, line, g)
    g = g * (weight * s) * s_col
    eye = (row == col).astype(jnp.float32)
    done = eliminated(jnp.concatenate([g, eye, jnp.zeros((32, 64), jnp.float32)], 1))
    factor[...] = jnp.where(col >= row, done[:, :32], 0.0)
    l = jnp.where(col <= row, done[:, 32:64], 0.0)
    diagonal[...] = jnp.broadcast_to(l[31:32, 31:32], diagonal.shape)
    scaled = jnp.where(col < 31, l * s, 0.0)
    hi = scaled.astype(jnp.bfloat16)
    lo = (scaled - hi.astype(jnp.float32)).astype(jnp.bfloat16)
    left = group_matrix((256, 32), 0, jnp.bfloat16)
    right = group_matrix((32, 256), 1, jnp.bfloat16)
    keep = same_layer()
    for part, out in ((hi, high), (lo, low)):
        wide = jnp.dot(left, part, preferred_element_type=jnp.float32)
        wide = jnp.dot(
            wide.astype(jnp.bfloat16), right, preferred_element_type=jnp.float32
        )
        out[...] = jnp.where(keep, wide, 0.0).astype(jnp.bfloat16)


EARLY = 6


def modes_kernel(
    weight,
    parts,
    scale,
    merged_a,
    merged_b,
    newest,
    modes,
    factor,
    merged,
    out,
    high,
    low,
    diagonal,
    in_sems,
    out_sems,
):
    width = newest.shape[-1] // 2
    pieces = [(3 * i + c, i, c) for i in range(2) for c in range(3)]
    loads = [
        pltpu.make_async_copy((merged_a, merged_b)[i].at[c], merged.at[n], in_sems.at[n])
        for n, i, c in pieces
    ]
    for load in loads[:EARLY]:
        load.start()
    weights_of(weight, parts, scale, factor, high, low, diagonal)
    for load in loads[EARLY:]:
        load.start()
    stores = []
    for n, i, c in pieces:
        loads[n].wait()
        at = slice(i * width, (i + 1) * width)
        rows = merged[n]
        value = jnp.dot(high[...], rows, preferred_element_type=jnp.float32)
        value = value + jnp.dot(low[...], rows, preferred_element_type=jnp.float32)
        value = value.reshape(32, 8, width)
        out[:31, c, :, at] = value[:31].astype(jnp.bfloat16)
        own = diagonal[:, :1] * newest[c, :, at]
        out[31, c, :, at] = (value[31] + own).astype(jnp.bfloat16)
        store = pltpu.make_async_copy(
            out.at[:, c, :, at], modes.at[:, c, :, at], out_sems.at[n]
        )
        store.start()
        stores.append(store)
    for store in stores:
        store.wait()


def modes_call(parts, scale, merged, newest, weight):
    length = newest.shape[-1]
    shape = (32, 3, 8, length)
    hbm = pl.BlockSpec(memory_space=pltpu.HBM)
    return call(
        functools.partial(modes_kernel, weight),
        (jax.ShapeDtypeStruct(shape, jnp.bfloat16), f32(32, 32)),
        (parts, scale, *in_hbm(*merged), newest),
        [
            pltpu.VMEM((6, 256, length // 2), jnp.bfloat16),
            pltpu.VMEM(shape, jnp.bfloat16),
            pltpu.VMEM((256, 256), jnp.bfloat16),
            pltpu.VMEM((256, 256), jnp.bfloat16),
            pltpu.VMEM((8, LANES), jnp.float32),
            pltpu.SemaphoreType.DMA((6,)),
            pltpu.SemaphoreType.DMA((6,)),
        ],
        in_specs=[WHOLE, WHOLE, hbm, hbm, WHOLE],
        out_specs=[hbm, WHOLE],
        flops=4 * 256 * 256 * 3 * length,
        nbytes=63 * 3 * 8 * length * 2,
    )


def shifted(block, axis, distance):
    count = lax.axis_size(axis)
    route = [(i, (i + distance) % count) for i in range(count)]
    return lax.ppermute(block, axis, route)


def exchange(sends):
    to_far, to_near, first_y, last_y = sends
    count = lax.axis_size("gx")
    pairs = [(i, (i + 1) % count) for i in range(1, count, 2)]
    far = lax.ppermute(to_far, "gx", pairs + [(j, i) for i, j in pairs])
    near = lax.ppermute(to_near, "gx", [(i, i ^ 1) for i in range(count)])
    before = shifted(last_y, "gy", 1)
    after = shifted(first_y, "gy", -1)
    return (far, near, before, after)


def total_parts(part):
    count, other = lax.axis_size("gx"), lax.axis_size("gy")
    part = part + lax.ppermute(part, "gx", [(i, i ^ 1) for i in range(count)])
    groups = [
        [i for i in range(count * other) if i // other % 2 == core] for core in range(2)
    ]
    copies = jnp.broadcast_to(part[None], (count * other // 2, *part.shape))
    return lax.all_to_all(
        copies, ("gx", "gy"), 0, 0, tiled=True, axis_index_groups=groups
    )


def local(density, momentum, energy, basis, scales, snapshots):
    rows, length = density.shape
    devices = lax.axis_size("gx") * lax.axis_size("gy")
    weight = 1.0 / (3 * rows * length * devices)
    fields = (density, momentum, energy)
    scale = jnp.concatenate([scales, jnp.ones((16,), jnp.float32)])[None]

    odd = (lax.axis_index("gx") % 2).astype(jnp.int32)[None]
    fields, along_z, sends = pack(odd, fields)
    state, old = fields, []
    for stage in range(3):
        halo, inner = exchange(sends), inner_call(along_z, state)
        if stage < 2:
            old.append(gram_call(basis, snapshots, stage))
            halo, inner, old = lax.optimization_barrier((halo, inner, old))
        state, sends = outer_call(stage, odd, inner, halo, state, fields)
    final, (newest,) = state, sends
    grams, merged = zip(*old)
    parts = total_parts(cross_call(merged, newest, grams))
    modes, factor = modes_call(parts, scale, merged, newest, weight)
    return (final[0], final[1], final[2], modes, factor)


def solution(mesh):
    field, vector = P("gx", "gy"), P(None, "gx", "gy")
    columns = P(None, None, "gx", "gy")
    return jax.shard_map(
        local,
        mesh=mesh,
        in_specs=(field, vector, field, columns, P(), columns),
        out_specs=(field, vector, field, columns, P()),
        check_vma=False,
    )
```
